32 devices in a mesh: grp: 4 (over z), loc: 8 (over y, x, core).
Axes of the slice: x: 2, y: 2, z: 4, core: 2. Of those that a mesh axis runs over, the one named last changes fastest.
Arguments:
- fields: float32 [512, 4, 512], P(('grp', 'loc')), may hold values from 0 to 1
- target: int32 [512], P(('grp', 'loc')), may hold values from 0 to 127, as said below
- gradient_matrix: float32 [4, 4], replicated, may hold values from -0.05 to 0.4, as said below
- relaxation: float32 [4], replicated, may hold values from 0.04 to 0.2
- interaction: float32 [3, 4, 4], replicated, may hold values from -4 to 4
Outputs:
- evolved: float32 [512, 4, 512], P(('grp', 'loc'))
The draws below stay inside these ranges and needn't reach their ends.
Inputs may be any that keep to these rules, and one draw needn't show every extreme that they name: Within each group, target maps the old slots one to one onto the new slots. One device sends at most 2 patches to each device of its group and receives at most 2 from each; every device sends exactly 2 patches to each device it sends to. The new slot number depends only on the group and the old slot number. `gradient_matrix`: diagonal entries lie between 0.2 and 0.4, the others between -0.05 and 0.05.
All inputs are finite; a program needn't handle non-finite values.
Results may differ from the reference program's by a relative error of at most 0.00002.
Values sent between devices are 32-bit elements; how exact they have to be, the bound alone decides.
No kernel may reach another device: no remote copies, remote signals or barrier semaphores. Data moves between devices by JAX's collectives and lax.ppermute only.
A program may use at most 64 MiB of HBM per device.

```python
import math
import jax
import jax.numpy as jnp
from jax import lax

COMP = 4
B = 8
PX = 16
PZ = 1
S = 16
PATCHES = 512
N_GRP = 4
N_LOC = 8


def target_group(group_key):
    slot_count = PX * PZ
    capacity = (slot_count + N_LOC - 1) // N_LOC
    group_keys = jax.random.split(group_key, 4)
    relabel = jax.random.permutation(group_keys[0], N_LOC)
    inverse = jnp.argsort(relabel)
    offsets = jax.random.permutation(group_keys[1], N_LOC)
    ordering = jax.random.permutation(group_keys[2], slot_count)
    slot_map = jax.random.permutation(group_keys[3], slot_count)
    displace = offsets[ordering // capacity]
    senders = jnp.arange(N_LOC)[:, None]
    receiver = inverse[(relabel[senders] + displace[None, :]) % N_LOC]
    return (receiver * slot_count + slot_map[None, :]).reshape(-1).astype(jnp.int32)


def draw_target(key, part):
    key = jax.random.fold_in(key, 11)
    group_keys = jax.random.split(key, N_GRP)
    return jax.vmap(target_group)(group_keys).reshape(-1).astype(jnp.int32)


def draw_gradient_matrix(key, part):
    key = jax.random.fold_in(key, 23)
    split_keys = jax.random.split(key, 2)
    uniform_diag = jax.random.uniform(split_keys[0], (COMP,), jnp.float32)
    uniform_off = jax.random.uniform(split_keys[1], (COMP, COMP), jnp.float32)
    diagonal = 0.2 + 0.2 * uniform_diag
    off_diagonal = 0.1 * uniform_off - 0.05
    identity = jnp.eye(COMP, dtype=jnp.float32)
    return (off_diagonal * (1.0 - identity) + identity * diagonal[None, :]).astype(jnp.float32)


def block_scale(key, dims, cuts, smallest, largest):
    def one(dim, blocks):
        steps = jax.random.uniform(jax.random.fold_in(jax.random.fold_in(key, 6), dim), (blocks,), jnp.float32, smallest / len(cuts), largest / len(cuts))
        return jnp.repeat(jnp.exp(steps), dims[dim] // blocks).reshape((-1,) + (1,) * (len(dims) - dim - 1))

    factor_of = one(*cuts[0])
    for cut in cuts[1:]:
        factor_of = factor_of * one(*cut)
    return factor_of


def bell_draw(rng, extent, scale, bound, kind=jnp.bfloat16):
    entries = scale * jax.random.normal(rng, extent, jnp.float32)
    return jnp.clip(entries, min=-bound, max=bound).astype(kind)


def setup_inputs(seed: int = 0) -> dict:
    keys = jax.random.split(jax.random.key(seed), 6)
    return {
        "fields": jnp.clip(1.0 * jax.random.uniform(keys[0], (PATCHES, COMP, B * B * B), jnp.float32) ** block_scale(keys[0], (PATCHES, COMP, B * B * B), ((0, 32),), -0.2, 0.2), 0.0, 1.0),
        "target": draw_target(jax.random.fold_in(keys[5], 71), 0),
        "gradient_matrix": draw_gradient_matrix(jax.random.fold_in(keys[5], 71), 0),
        "relaxation": jnp.clip(jnp.exp(jax.random.uniform(keys[3], (COMP,), jnp.float32, math.log(0.04), math.log(0.2))), 0.04, 0.2),
        "interaction": bell_draw(keys[4], (3, COMP, COMP), 1.0, 4.0, jnp.float32),
    }


def reaction(components, interaction):
    count_comp = len(components)
    partials = [jnp.zeros_like(components[0]) for first_index in range(count_comp)]
    for first_index in range(count_comp):
        for second_index in range(first_index + 1, count_comp):
            first_conc = components[first_index]
            second_conc = components[second_index]
            spread_gap = first_conc - second_conc
            energy_poly = interaction[0, first_index, second_index] + interaction[1, first_index, second_index] * spread_gap + interaction[2, first_index, second_index] * spread_gap * spread_gap
            slope_term = interaction[1, first_index, second_index] + 2.0 * interaction[2, first_index, second_index] * spread_gap
            cross_term = first_conc * second_conc * slope_term
            partials[first_index] = partials[first_index] + second_conc * energy_poly + cross_term
            partials[second_index] = partials[second_index] + first_conc * energy_poly - cross_term
    return partials


def stacked_reaction(block_cells, interaction):
    return jnp.stack(reaction([block_cells[number] for number in range(block_cells.shape[0])], interaction))


def second_difference(values, along):
    length = values.shape[along]

    def shifted(offset):
        return lax.slice_in_dim(values, 2 + offset, length - 2 + offset, axis=along)

    return (16.0 * (shifted(-1) + shifted(1)) - (shifted(-2) + shifted(2)) - 30.0 * shifted(0)) / 12.0


def periodic_difference(values, along):
    return (16.0 * (jnp.roll(values, 1, along) + jnp.roll(values, -1, along)) - (jnp.roll(values, 2, along) + jnp.roll(values, -2, along)) - 30.0 * values) / 12.0


def advance(padded_block, chemical, gradient_matrix, relaxation):
    center = padded_block[:, 2:-2, 2:-2]
    z_lap = second_difference(padded_block[:, :, 2:-2], 1)
    y_lap = second_difference(padded_block[:, 2:-2], 2)
    x_lap = periodic_difference(center, 3)
    laplace = z_lap + y_lap + x_lap
    smooth_terms = []
    for first_index in range(padded_block.shape[0]):
        running = gradient_matrix[first_index, 0] * laplace[0]
        for second_index in range(1, padded_block.shape[0]):
            running = running + gradient_matrix[first_index, second_index] * laplace[second_index]
        smooth_terms.append(running)
    return center - relaxation[:, None, None, None] * (chemical - jnp.stack(smooth_terms))


def deposit_group(slot_data, destinations):
    return jnp.zeros_like(slot_data).at[destinations].set(slot_data)


def reference(fields, target, gradient_matrix, relaxation, interaction):
    per_group = S * N_LOC
    cell_count = B * B * B
    old_slots = fields.reshape(N_GRP, per_group, COMP, cell_count)
    targets = target.reshape(N_GRP, per_group)
    migrated = jax.vmap(deposit_group)(old_slots, targets)
    cell_grid = migrated.reshape(N_GRP, N_LOC, PZ, PX, COMP, B, B, B).transpose(4, 0, 2, 5, 1, 6, 3, 7)
    cell_grid = cell_grid.reshape(COMP, N_GRP * PZ * B, N_LOC * B, PX * B)
    slab_depth = PZ * B
    wrapped = jnp.concatenate([cell_grid[:, -4:], cell_grid, cell_grid[:, :4]], axis=1)

    def one_group(group_index):
        group_slab = lax.dynamic_slice_in_dim(wrapped, group_index * slab_depth, slab_depth + 8, axis=1)
        group_slab = jnp.concatenate([group_slab[:, :, -4:], group_slab, group_slab[:, :, :4]], axis=2)
        for repeat in range(2):
            inner_cells = group_slab[:, 2:-2, 2:-2]
            group_slab = advance(group_slab, stacked_reaction(inner_cells, interaction), gradient_matrix, relaxation)
        group_slab = group_slab.reshape(COMP, PZ, B, N_LOC, B, PX, B).transpose(3, 1, 5, 0, 2, 4, 6)
        return group_slab.reshape(per_group, COMP, cell_count)

    result = lax.map(one_group, jnp.arange(N_GRP, dtype=jnp.int32))
    return result.reshape(N_GRP * per_group, COMP, cell_count)
```

```python
import jax
import jax.numpy as jnp
from jax import lax
from jax.experimental import pallas as pl
from jax.experimental.pallas import tpu as pltpu
from jax.sharding import PartitionSpec as P

COMP = 4
LANES = 128
CHUNKS = 4
ROWS = CHUNKS * COMP
TOP = 8
DEPTH = 32

VMEM = pl.BlockSpec(memory_space=pltpu.VMEM)
SMEM = pl.BlockSpec(memory_space=pltpu.SMEM)


def lane_parts(shape):
    lane = lax.broadcasted_iota(jnp.int32, shape, 1)
    return lane // 64, (lane // 8) % 8, lane % 8


def pack_kernel(peers, cap, slots, target, fields, out, count, held, label):
    for peer in range(peers):
        count[peer] = 0
        for k in range(cap):
            held[peer * cap + k] = 0
            label[peer * cap + k] = slots
    for i in range(slots):
        goal = target[i]
        peer = lax.div(goal, slots)
        k = count[peer]
        count[peer] = k + 1
        held[peer * cap + k] = i
        label[peer * cap + k] = lax.rem(goal, slots)
    _, y, _ = lane_parts((COMP, LANES))
    row = lax.broadcasted_iota(jnp.int32, (8, LANES), 1)
    for peer in range(peers):
        after, before = (peer + 1) % peers, (peer - 1) % peers
        names = jnp.zeros((8, LANES), jnp.int32)
        for k in range(cap):
            own, high, low = held[peer * cap + k], held[after * cap + k], held[before * cap + k]
            names = jnp.where(row == k, label[peer * cap + k], names)
            names = jnp.where(row == cap + k, label[after * cap + k], names)
            names = jnp.where(row == 2 * cap + k, label[before * cap + k], names)
            for chunk in range(CHUNKS):
                part = slice(chunk * LANES, (chunk + 1) * LANES)
                at = k * ROWS + chunk * COMP
                out[peer, at : at + COMP, :] = fields[own, :, part]
                at += cap * ROWS
                out[peer, at : at + COMP, :] = jnp.where(y < 4, fields[high, :, part], fields[low, :, part])
        out[peer, 2 * cap * ROWS :, :] = names.astype(jnp.float32)


def place_kernel(peers, cap, slots, got, block, high, low, up, down):
    half = ROWS // 2
    _, y, _ = lane_parts((COMP, LANES))
    for peer in range(peers):
        names = got[peer, 2 * cap * ROWS : 2 * cap * ROWS + 1, :].astype(jnp.int32)
        for k in range(cap):
            slot = names[0, k]
            index = jnp.where(slot == slots, slots + 2, slot + 1)
            block[index] = got[peer, k * ROWS : (k + 1) * ROWS, :]
            joined = got[peer, (cap + k) * ROWS : (cap + k + 1) * ROWS, :]
            high[names[0, cap + k]] = joined
            low[names[0, 2 * cap + k]] = joined
    block[0] = block[slots]
    block[slots + 1] = block[1]
    up[: slots + 2] = block[: slots + 2, half:, :]
    down[: slots + 2] = block[: slots + 2, :half, :]
    last = ROWS - COMP
    for t in range(slots):
        at = (t % 2) * COMP
        up[slots + 2 + t // 2, at : at + COMP, :] = jnp.where(y < 4, high[t, last:, :], low[t, last:, :])
        down[slots + 2 + t // 2, at : at + COMP, :] = jnp.where(y < 4, high[t, :COMP, :], low[t, :COMP, :])


def turn(v, shift):
    return pltpu.roll(v, shift % LANES, 1)


def step(v, ahead, behind, above, below, beside, scalars):
    rates, mixing, pairs = scalars
    layer, y, x = lane_parts(v[0].shape)
    laps = []
    for c in range(COMP):
        near = turn(jnp.where(layer == 0, above[c], v[c]), 64) + turn(jnp.where(layer == 0, v[c], below[c]), 64)
        far = above[c] + below[c]
        other = turn(beside[c], 64)
        near += turn(jnp.where(y == 0, other, v[c]), -8) + turn(jnp.where(y == 7, other, v[c]), 8)
        far += turn(jnp.where(y < 2, other, v[c]), -16) + turn(jnp.where(y >= 6, other, v[c]), 16)
        plus, minus = turn(ahead[c], 8), turn(behind[c], -8)
        near += turn(jnp.where(x == 0, plus, v[c]), -1) + turn(jnp.where(x == 7, minus, v[c]), 1)
        far += turn(jnp.where(x < 2, plus, v[c]), -2) + turn(jnp.where(x >= 6, minus, v[c]), 2)
        laps.append(16.0 * near - far - 90.0 * v[c])
    drive = [None] * COMP
    for (i, j), (a, b, c) in pairs.items():
        gap = v[i] - v[j]
        bend = c * gap
        slope = b + bend
        energy = a + slope * gap
        cross = v[i] * v[j] * (slope + bend)
        first = v[j] * energy + cross
        second = v[i] * energy - cross
        drive[i] = first if drive[i] is None else drive[i] + first
        drive[j] = second if drive[j] is None else drive[j] + second
    result = []
    for i in range(COMP):
        total = v[i] - rates[i] * drive[i]
        for j in range(COMP):
            total += mixing[i][j] * laps[j]
        result.append(total)
    return result


def evolve_kernel(slots, block, high, low, below, above, gradient, relaxation, interaction, out, first, first_side, second, second_side):
    rows = slice(TOP, TOP + slots)
    rates = [relaxation[i] for i in range(COMP)]
    mixing = [[rates[i] * gradient[i, j] * (1.0 / 12.0) for j in range(COMP)] for i in range(COMP)]
    pairs = {
        (i, j): (interaction[0, i, j], interaction[1, i, j], interaction[2, i, j])
        for i in range(COMP)
        for j in range(i + 1, COMP)
    }
    scalars = rates, mixing, pairs
    half = ROWS // 2
    _, y, _ = lane_parts((slots, LANES))

    def ringed(ref, at, c, value):
        ref[at, c, rows, :] = value
        ref[at, c, TOP - 1 : TOP, :] = value[slots - 1 :]
        ref[at, c, TOP + slots : TOP + slots + 1, :] = value[:1]

    def column(ref, start, row):
        flat = ref.reshape(ref.shape[0] * ref.shape[1], LANES)
        return flat[pl.ds(start * ref.shape[1] + row, slots, stride=ref.shape[1]), :]

    def side_column(ref, c):
        flat = ref.reshape(ref.shape[0] * ref.shape[1], LANES)
        return flat[pl.ds((slots + 2) * half + c, slots, stride=COMP), :]

    for c in range(COMP):
        for chunk in range(CHUNKS):
            ringed(first, chunk + 2, c, column(block, 1, chunk * COMP + c))
            ringed(
                first_side,
                chunk + 1,
                c,
                jnp.where(y < 4, column(high, 0, chunk * COMP + c), column(low, 0, chunk * COMP + c)),
            )
        for chunk in range(2):
            ringed(first, chunk, c, column(below, 1, chunk * COMP + c))
            ringed(first, chunk + 6, c, column(above, 1, chunk * COMP + c))
        first_side[0, c, rows, :] = side_column(below, c)
        first_side[5, c, rows, :] = side_column(above, c)

    def take(ref, at, offset=0):
        return [ref[at, c, TOP + offset : TOP + offset + slots, :] for c in range(COMP)]

    def moved(ref, at, side):
        return step(take(ref, at), take(ref, at, 1), take(ref, at, -1), take(ref, at + 1), take(ref, at - 1), side, scalars)

    @pl.loop(0, CHUNKS + 2)
    def _(k):
        for c, value in enumerate(moved(first, k + 1, take(first_side, k))):
            ringed(second, k, c, value)

    @pl.loop(0, CHUNKS)
    def _(k):
        for c, value in enumerate(moved(first_side, k + 1, take(first, k + 2))):
            second_side[k, c, rows, :] = value

    @pl.loop(0, CHUNKS)
    def _(k):
        for c, value in enumerate(moved(second, k + 1, take(second_side, k))):
            out[:, c, pl.ds(pl.multiple_of(k * LANES, LANES), LANES)] = value


def per_device(fields, target, gradient_matrix, relaxation, interaction):
    slots = fields.shape[0]
    peers = lax.axis_size("loc")
    groups = lax.axis_size("grp")
    cap = (slots + peers - 1) // peers
    half = ROWS // 2
    f32 = jnp.float32

    def shape(*dims):
        return jax.ShapeDtypeStruct(dims, f32)

    sent = pl.pallas_call(
        lambda *refs: pack_kernel(peers, cap, slots, *refs),
        out_shape=shape(peers, 2 * cap * ROWS + 8, LANES),
        in_specs=[SMEM, VMEM],
        out_specs=VMEM,
        scratch_shapes=[
            pltpu.SMEM((peers,), jnp.int32),
            pltpu.SMEM((peers * cap,), jnp.int32),
            pltpu.SMEM((peers * cap,), jnp.int32),
        ],
        name="pack",
    )(target, fields)
    got = lax.all_to_all(sent, "loc", split_axis=0, concat_axis=0, tiled=True)
    block, high, low, up, down = pl.pallas_call(
        lambda *refs: place_kernel(peers, cap, slots, *refs),
        out_shape=(
            shape(slots + 3, ROWS, LANES),
            shape(slots + 1, ROWS, LANES),
            shape(slots + 1, ROWS, LANES),
            shape(slots + 2 + slots // 2, half, LANES),
            shape(slots + 2 + slots // 2, half, LANES),
        ),
        in_specs=[VMEM],
        out_specs=(VMEM,) * 5,
        name="place",
    )(got)
    forward = [(i, (i + 1) % groups) for i in range(groups)]
    backward = [(j, i) for i, j in forward]
    below = lax.ppermute(up, "grp", forward)
    above = lax.ppermute(down, "grp", backward)
    return pl.pallas_call(
        lambda *refs: evolve_kernel(slots, *refs),
        out_shape=shape(*fields.shape),
        in_specs=[VMEM] * 5 + [SMEM] * 3,
        out_specs=VMEM,
        scratch_shapes=[
            pltpu.VMEM((CHUNKS + 4, COMP, DEPTH, LANES), f32),
            pltpu.VMEM((CHUNKS + 2, COMP, DEPTH, LANES), f32),
            pltpu.VMEM((CHUNKS + 2, COMP, DEPTH, LANES), f32),
            pltpu.VMEM((CHUNKS, COMP, DEPTH, LANES), f32),
        ],
        name="evolve",
    )(block, high, low, below, above, gradient_matrix, relaxation, interaction)


def solution(mesh):
    placed = (P(("grp", "loc"), None, None), P(("grp", "loc")), P(), P(), P())
    return jax.shard_map(
        per_device,
        mesh=mesh,
        in_specs=placed,
        out_specs=P(("grp", "loc"), None, None),
        check_vma=False,
    )
```

```python
import jax
import jax.numpy as jnp
from jax import lax
from jax.experimental import pallas as pl
from jax.experimental.pallas import tpu as pltpu
from jax.sharding import PartitionSpec as P

COMP = 4
LANES = 128
CHUNKS = 4
ROWS = CHUNKS * COMP
HALF = ROWS // 2
TOP = 8
DEPTH = 32
PAIRS = [(i, j) for i in range(COMP) for j in range(i + 1, COMP)]
TABLE = COMP + COMP * COMP + 3 * len(PAIRS)

VMEM = pl.BlockSpec(memory_space=pltpu.VMEM)
SMEM = pl.BlockSpec(memory_space=pltpu.SMEM)


def lane_parts(shape):
    lane = lax.broadcasted_iota(jnp.int32, shape, 1)
    return lane // 64, (lane // 8) % 8, lane % 8


def turn(v, shift):
    return pltpu.roll(v, shift % LANES, 1)


def pack_kernel(peers, cap, slots, target, other_target, fields, other_fields, *refs):
    outs, (count, held, label) = refs[: peers // 2], refs[peers // 2 :]
    for core, goals in enumerate((target[...], other_target[...])):
        for peer in range(peers):
            count[core * peers + peer] = 0
            for k in range(cap):
                held[(core * peers + peer) * cap + k] = 0
                label[(core * peers + peer) * cap + k] = slots
        for i in range(slots):
            goal = goals[0, i]
            peer = core * peers + lax.div(goal, slots)
            k = count[peer]
            count[peer] = k + 1
            held[peer * cap + k] = i
            label[peer * cap + k] = lax.rem(goal, slots)
    _, y, _ = lane_parts((COMP, LANES))
    row = lax.broadcasted_iota(jnp.int32, (8, LANES), 1)
    me = lax.axis_index("loc")
    for j, out in enumerate(outs):
        peer = me ^ (2 * j)
        places = [lax.rem(peer + d, peers) * cap for d in (0, 1, peers - 1)]
        names = jnp.zeros((8, LANES), jnp.int32)
        for core, source in enumerate((fields, other_fields)):
            for k in range(cap):
                own, high, low = [held[core * peers * cap + at + k] for at in places]
                entry = core * cap + k
                for n, at in enumerate(places):
                    names = jnp.where(row == 2 * cap * n + entry, label[core * peers * cap + at + k], names)
                for chunk in range(CHUNKS):
                    part = slice(chunk * LANES, (chunk + 1) * LANES)
                    at = entry * ROWS + chunk * COMP
                    out[at : at + COMP, :] = source[own, :, part]
                    at += 2 * cap * ROWS
                    out[at : at + COMP, :] = jnp.where(y < 4, source[high, :, part], source[low, :, part])
        out[4 * cap * ROWS :, :] = names.astype(jnp.float32)


def entries(cap, got):
    for message in got:
        names = message[4 * cap * ROWS : 4 * cap * ROWS + 1, :].astype(jnp.int32)
        for k in range(2 * cap):
            yield message, k * ROWS, (2 * cap + k) * ROWS, names[0, k], names[0, 2 * cap + k], names[0, 4 * cap + k]


def faces_kernel(cap, slots, *refs):
    got, (up, down, high, low) = refs[:-4], refs[-4:]
    _, y, _ = lane_parts((2 * COMP, LANES))
    for message, whole, joined, slot, high_slot, low_slot in entries(cap, got):
        down[slot] = message[whole : whole + HALF, :]
        up[slot] = message[whole + HALF : whole + ROWS, :]
        for part, at in ((0, 0), (COMP, ROWS - COMP)):
            rows = message[joined + at : joined + at + COMP, :]
            high[high_slot, part : part + COMP, :] = rows
            low[low_slot, part : part + COMP, :] = rows
    pairs = slots // 2
    for q in range(pairs):
        one, two = [jnp.where(y < 4, high[t], low[t]) for t in (q, q + pairs)]
        two = jnp.where(y < 4, turn(two, 16), turn(two, -16))
        both = jnp.where((y >= 2) & (y < 6), two, one)
        at = (q % 2) * COMP
        down[slots + 1 + q // 2, at : at + COMP, :] = both[:COMP]
        up[slots + 1 + q // 2, at : at + COMP, :] = both[COMP:]


def stage_kernel(fields, target, gradient, relaxation, interaction, out, goals, table):
    out[...] = fields[...]
    goals[...] = target[...]
    for i in range(COMP):
        rate = relaxation[i]
        table[i] = rate
        for j in range(COMP):
            table[COMP + i * COMP + j] = rate * gradient[i, j] * (1.0 / 12.0)
    at = COMP + COMP * COMP
    for i, j in PAIRS:
        for order in range(3):
            table[at] = interaction[order, i, j]
            at += 1


def coefficients(table):
    rates = [table[i] for i in range(COMP)]
    mixing = [[table[COMP + i * COMP + j] for j in range(COMP)] for i in range(COMP)]
    at = COMP + COMP * COMP
    pairs = {pair: [table[at + 3 * n + order] for order in range(3)] for n, pair in enumerate(PAIRS)}
    return rates, mixing, pairs


def mixed(start, laps, mixing):
    result = []
    for i in range(COMP):
        total = start[i]
        for j in range(COMP):
            total += mixing[i][j] * laps[j]
        result.append(total)
    return result


def step(v, ahead, behind, above, below, beside, scalars):
    rates, mixing, pairs = scalars
    layer, y, x = lane_parts(v[0].shape)
    laps = []
    for c in range(COMP):
        near = turn(jnp.where(layer == 0, above[c], v[c]), 64) + turn(jnp.where(layer == 0, v[c], below[c]), 64)
        far = above[c] + below[c]
        other = turn(beside[c], 64)
        near += turn(jnp.where(y == 0, other, v[c]), -8) + turn(jnp.where(y == 7, other, v[c]), 8)
        far += turn(jnp.where(y < 2, other, v[c]), -16) + turn(jnp.where(y >= 6, other, v[c]), 16)
        plus, minus = turn(ahead[c], 8), turn(behind[c], -8)
        near += turn(jnp.where(x == 0, plus, v[c]), -1) + turn(jnp.where(x == 7, minus, v[c]), 1)
        far += turn(jnp.where(x < 2, plus, v[c]), -2) + turn(jnp.where(x >= 6, minus, v[c]), 2)
        laps.append(16.0 * near - far - 90.0 * v[c])
    drive = [None] * COMP
    for (i, j), (a, b, c) in pairs.items():
        gap = v[i] - v[j]
        bend = c * gap
        slope = b + bend
        energy = a + slope * gap
        cross = v[i] * v[j] * (slope + bend)
        first = v[j] * energy + cross
        second = v[i] * energy - cross
        drive[i] = first if drive[i] is None else drive[i] + first
        drive[j] = second if drive[j] is None else drive[j] + second
    return mixed([v[i] - rates[i] * drive[i] for i in range(COMP)], laps, mixing)


def store(slots, ref, at, values):
    for c, value in enumerate(values):
        ref[at, c, TOP : TOP + slots, :] = value
        ref[at, c, TOP - 1 : TOP, :] = value[slots - 1 :]
        ref[at, c, TOP + slots : TOP + slots + 1, :] = value[:1]


def load(slots, ref, at, offset=0):
    return [ref[at, c, TOP + offset : TOP + offset + slots, :] for c in range(COMP)]


def moved(slots, work, at, above, below, beside, scalars):
    ahead, behind = load(slots, work, at, 1), load(slots, work, at, -1)
    around = [load(slots, work, n) for n in (above, below, beside)]
    return step(load(slots, work, at), ahead, behind, *around, scalars)


def column(ref, start, count, stride):
    flat = ref.reshape(ref.shape[0] * ref.shape[1], LANES)
    return flat[pl.ds(start, count, stride=stride), :]


SPAN = CHUNKS + 2
BLOCK, SIDE, BLOCK_NEXT, SIDE_NEXT, FINAL, BELOW, ABOVE = [n * SPAN for n in range(5)] + [4 * SPAN + 2, 4 * SPAN + 3]
ENTRIES = ABOVE + 1


def inner_kernel(cap, slots, peers, *refs):
    got, (table, work, block, high, low) = refs[: peers // 2], refs[peers // 2 :]
    scalars = coefficients(table)
    _, y, _ = lane_parts((slots, LANES))
    for message, whole, joined, slot, high_slot, low_slot in entries(cap, got):
        block[slot] = message[whole : whole + ROWS, :]
        rows = message[joined : joined + ROWS, :]
        high[high_slot] = rows
        low[low_slot] = rows
    for base in range(0, FINAL, SPAN):
        for at in (base, base + SPAN - 1):
            work[at] = jnp.zeros(work.shape[1:], work.dtype)

    @pl.loop(0, CHUNKS)
    def _(k):
        rows = [k * COMP + c for c in range(COMP)]
        store(slots, work, BLOCK + 1 + k, [column(block, r, slots, ROWS) for r in rows])
        sides = [jnp.where(y < 4, column(high, r, slots, ROWS), column(low, r, slots, ROWS)) for r in rows]
        store(slots, work, SIDE + 1 + k, sides)

    @pl.loop(0, 2 * CHUNKS + 2)
    def _(n):
        late = n >= 2 * CHUNKS
        side = n // CHUNKS
        k = n % CHUNKS
        at = jnp.where(late, BLOCK_NEXT + 2 + k, side * SPAN + 1 + k)
        above = jnp.where(n == 2 * CHUNKS + 1, BLOCK_NEXT + SPAN - 1, at + 1)
        below = jnp.where(n == 2 * CHUNKS, BLOCK_NEXT, at - 1)
        beside = jnp.where(late, SIDE_NEXT + 2 + k, (1 - side) * SPAN + 1 + k)
        to = jnp.where(late, FINAL + k, BLOCK_NEXT + side * SPAN + 1 + k)
        store(slots, work, to, moved(slots, work, at, above, below, beside, scalars))


def finish(slots, end, ref, table, work, target):
    scalars = coefficients(table)
    mixing = scalars[1]
    pairs = slots // 2
    _, y, _ = lane_parts((pairs, LANES))
    layer, _, _ = lane_parts((slots, LANES))
    outside, edge = end * (SPAN - 1), 1 + end * (CHUNKS - 1)
    near, distant, side = [], [], []
    for c in range(COMP):
        near.append(column(ref, (1 - end) * COMP + c, slots, HALF))
        distant.append(column(ref, end * COMP + c, slots, HALF))
        both = column(ref, (slots + 1) * HALF + c, pairs, COMP)
        side.append(jnp.concatenate([both, jnp.where(y < 4, turn(both, -16), turn(both, 16))], axis=0))
    store(slots, work, BLOCK + outside, near)
    store(slots, work, ABOVE if end else BELOW, distant)
    store(slots, work, SIDE + outside, side)

    @pl.loop(0, 3)
    def _(kind):
        source = jnp.where(kind == 2, BLOCK_NEXT + edge, kind * SPAN + outside)
        to = jnp.where(kind == 2, FINAL + end, BLOCK_NEXT + kind * SPAN + edge)
        laps = [16.0 * turn(jnp.where(layer == 1 - end, b, 0.0), 64) - b for b in load(slots, work, source)]
        store(slots, work, to, mixed(load(slots, work, to), laps, mixing))

    @pl.loop(0, 2)
    def _(late):
        at = jnp.where(late, BLOCK_NEXT + edge, BLOCK + outside)
        beyond = jnp.where(late, BLOCK_NEXT + outside, ABOVE if end else BELOW)
        within = at + 1 - 2 * end
        beside = jnp.where(late, SIDE_NEXT + edge, SIDE + outside)
        to = jnp.where(late, BLOCK + end, BLOCK_NEXT + outside)
        above, below = (beyond, within) if end else (within, beyond)
        store(slots, work, to, moved(slots, work, at, above, below, beside, scalars))

    results = [load(slots, work, FINAL + 1), load(slots, work, BLOCK + 1)] if end else [load(slots, work, BLOCK), load(slots, work, FINAL)]

    for k, values in enumerate(results):
        for c, value in enumerate(values):
            target[:, c, k * LANES : (k + 1) * LANES] = value


def lower_kernel(slots, ref, table, _, half, work):
    finish(slots, 0, ref, table, work, half)


def upper_kernel(slots, ref, table, lower, _, out, work, half, sems):
    length = half.shape[2]
    first = pltpu.make_async_copy(lower, out.at[:, :, :length], sems.at[0])
    first.start()
    finish(slots, 1, ref, table, work, half)
    last = pltpu.make_async_copy(half, out.at[:, :, length:], sems.at[1])
    last.start()
    first.wait()
    last.wait()


def per_device(fields, target, gradient_matrix, relaxation, interaction):
    slots = fields.shape[0]
    peers = lax.axis_size("loc")
    groups = lax.axis_size("grp")
    cap = (slots + peers - 1) // peers
    chips = peers // 2
    f32 = jnp.float32
    params = pltpu.CompilerParams(vmem_limit_bytes=8 << 20)

    def shape(*dims):
        return pltpu.VMEM(dims, f32)

    def inside(*arrays):
        return [pltpu.with_memory_space_constraint(a, pltpu.VMEM) for a in arrays]

    def cross(array, flip):
        return lax.ppermute(array, "loc", [(i, i ^ flip) for i in range(peers)])

    target = target.reshape(1, slots)
    staged, goals, table = pl.pallas_call(
        stage_kernel,
        out_shape=(shape(*fields.shape), pltpu.VMEM(target.shape, jnp.int32), pltpu.SMEM((TABLE,), f32)),
        in_specs=[VMEM] * 2 + [SMEM] * 3,
        out_specs=(VMEM, VMEM, SMEM),
        name="stage",
    )(fields, target, gradient_matrix, relaxation, interaction)
    table = pltpu.with_memory_space_constraint(table, pltpu.SMEM)
    other_fields, other_target = cross(fields, 1), cross(target, 1)
    sent = pl.pallas_call(
        lambda *refs: pack_kernel(peers, cap, slots, *refs),
        out_shape=(shape(4 * cap * ROWS + 8, LANES),) * chips,
        in_specs=[VMEM] * 4,
        out_specs=(VMEM,) * chips,
        scratch_shapes=[pltpu.SMEM((2 * peers * n,), jnp.int32) for n in (1, cap, cap)],
        name="pack",
        compiler_params=params,
    )(*inside(goals, other_target, staged, other_fields))
    got = inside(sent[0], *[cross(sent[j], 2 * j) for j in range(1, chips)])
    up, down = pl.pallas_call(
        lambda *refs: faces_kernel(cap, slots, *refs),
        out_shape=(shape(slots + 1 + slots // 4, HALF, LANES),) * 2,
        in_specs=[VMEM] * chips,
        out_specs=(VMEM,) * 2,
        scratch_shapes=[pltpu.VMEM((slots + 1, HALF, LANES), f32)] * 2,
        name="faces",
        compiler_params=params,
    )(*got)
    forward = [(i, (i + 1) % groups) for i in range(groups)]
    backward = [(j, i) for i, j in forward]
    below = lax.ppermute(up, "grp", forward)
    above = lax.ppermute(down, "grp", backward)
    work = pl.pallas_call(
        lambda *refs: inner_kernel(cap, slots, peers, *refs),
        out_shape=shape(ENTRIES, COMP, DEPTH, LANES),
        in_specs=[VMEM] * chips + [SMEM],
        out_specs=VMEM,
        scratch_shapes=[pltpu.VMEM((slots + 1, ROWS, LANES), f32)] * 3,
        name="inner",
        compiler_params=params,
    )(*got, table)
    half = (slots, COMP, fields.shape[2] // 2)
    lower, work = pl.pallas_call(
        lambda *refs: lower_kernel(slots, *refs),
        out_shape=(shape(*half), shape(*work.shape)),
        in_specs=[VMEM, SMEM, VMEM],
        out_specs=(VMEM,) * 2,
        input_output_aliases={2: 1},
        name="lower",
        compiler_params=params,
    )(*inside(below), table, *inside(work))
    return pl.pallas_call(
        lambda *refs: upper_kernel(slots, *refs),
        out_shape=(jax.ShapeDtypeStruct(fields.shape, f32), shape(*work.shape)),
        in_specs=[VMEM, SMEM, VMEM, VMEM],
        out_specs=(pl.BlockSpec(memory_space=pl.ANY), VMEM),
        input_output_aliases={3: 1},
        scratch_shapes=[pltpu.VMEM(half, f32), pltpu.SemaphoreType.DMA((2,))],
        name="upper",
        compiler_params=params,
    )(*inside(above), table, *inside(lower, work))[0]


def solution(mesh):
    placed = (P(("grp", "loc"), None, None), P(("grp", "loc")), P(), P(), P())
    return jax.shard_map(
        per_device,
        mesh=mesh,
        in_specs=placed,
        out_specs=P(("grp", "loc"), None, None),
        check_vma=False,
    )
```

```python
import jax
import jax.numpy as jnp
from jax import lax
from jax.experimental import pallas as pl
from jax.experimental.pallas import tpu as pltpu
from jax.sharding import PartitionSpec as P

COMP = 4
LANES = 128
CHUNKS = 4
ROWS = CHUNKS * COMP
HALF = ROWS // 2
TOP = 8
DEPTH = 32
PAIRS = [(i, j) for i in range(COMP) for j in range(i + 1, COMP)]
TABLE = COMP + COMP * COMP + 3 * len(PAIRS)

VMEM = pl.BlockSpec(memory_space=pltpu.VMEM)
SMEM = pl.BlockSpec(memory_space=pltpu.SMEM)


def lane_parts(shape):
    lane = lax.broadcasted_iota(jnp.int32, shape, 1)
    return lane // 64, (lane // 8) % 8, lane % 8


def turn(v, shift):
    return pltpu.roll(v, shift % LANES, 1)


def route_kernel(peers, cap, slots, target, other_target, held, label, count):
    for core, goals in enumerate((target[...], other_target[...])):
        for peer in range(peers):
            count[core * peers + peer] = 0
            for k in range(cap):
                held[(core * peers + peer) * cap + k] = 0
                label[(core * peers + peer) * cap + k] = slots
        for i in range(slots):
            goal = goals[0, i]
            peer = core * peers + lax.div(goal, slots)
            k = count[peer]
            count[peer] = k + 1
            held[peer * cap + k] = i
            label[peer * cap + k] = lax.rem(goal, slots)


def pack_kernel(peers, cap, flip, held, label, fields, other_fields, out, *weights):
    _, y, _ = lane_parts((COMP, LANES))
    row = lax.broadcasted_iota(jnp.int32, (8, LANES), 1)
    peer = lax.axis_index("loc") ^ flip
    places = [lax.rem(peer + d, peers) * cap for d in (0, 1, peers - 1)]
    names = jnp.zeros((8, LANES), jnp.int32)
    for core, source in enumerate((fields, other_fields)):
        for k in range(cap):
            own, high, low = [held[core * peers * cap + at + k] for at in places]
            entry = core * cap + k
            for n, at in enumerate(places):
                names = jnp.where(row == 2 * cap * n + entry, label[core * peers * cap + at + k], names)
            for chunk in range(CHUNKS):
                part = slice(chunk * LANES, (chunk + 1) * LANES)
                at = entry * ROWS + chunk * COMP
                out[at : at + COMP, :] = source[own, :, part]
                at += 2 * cap * ROWS
                out[at : at + COMP, :] = jnp.where(y < 4, source[high, :, part], source[low, :, part])
    out[4 * cap * ROWS :, :] = names.astype(jnp.float32)
    if weights:
        fill_weights(weights[0])


def fill_weights(out):
    shape = (LANES, LANES)
    z, y, x = lane_parts(shape)
    source = lax.broadcasted_iota(jnp.int32, shape, 0)
    dz, dy, dx = source // 64 - z, (source // 8) % 8 - y, source % 8 - x

    def stencil(d):
        return jnp.where(jnp.abs(d) == 1, 16.0, jnp.where(jnp.abs(d) == 2, -1.0, 0.0))

    def only(mask, value):
        return jnp.where(mask, value, 0.0)

    swap = only((dz != 0) & (dy == 0) & (dx == 0), 16.0)
    along_y, along_x = (dz == 0) & (dx == 0), (dz == 0) & (dy == 0)
    parts = (
        swap + only(along_y, stencil(dy)) + only(along_x, stencil(dx)),
        only(along_y, stencil(dy + 8) + stencil(dy - 8)),
        only(along_x, stencil(dx + 8) + stencil(dx - 8)),
        swap,
    )
    for n, part in enumerate(parts):
        out[n * LANES : (n + 1) * LANES, :] = part.astype(out.dtype)


def entries(cap, got):
    for message in got:
        names = message[4 * cap * ROWS : 4 * cap * ROWS + 1, :].astype(jnp.int32)
        for k in range(2 * cap):
            yield message, k * ROWS, (2 * cap + k) * ROWS, names[0, k], names[0, 2 * cap + k], names[0, 4 * cap + k]


def faces_kernel(cap, slots, *refs):
    got, (up, down, high, low) = refs[:-4], refs[-4:]
    _, y, _ = lane_parts((2 * COMP, LANES))
    for message, whole, joined, slot, high_slot, low_slot in entries(cap, got):
        down[slot] = message[whole : whole + HALF, :]
        up[slot] = message[whole + HALF : whole + ROWS, :]
        for part, at in ((0, 0), (COMP, ROWS - COMP)):
            rows = message[joined + at : joined + at + COMP, :]
            high[high_slot, part : part + COMP, :] = rows
            low[low_slot, part : part + COMP, :] = rows
    pairs = slots // 2
    for q in range(pairs):
        one, two = [jnp.where(y < 4, high[t], low[t]) for t in (q, q + pairs)]
        two = jnp.where(y < 4, turn(two, 16), turn(two, -16))
        both = jnp.where((y >= 2) & (y < 6), two, one)
        at = (q % 2) * COMP
        down[slots + q // 2, at : at + COMP, :] = both[:COMP]
        up[slots + q // 2, at : at + COMP, :] = both[COMP:]


def stage_kernel(fields, target, gradient, relaxation, interaction, out, goals, table):
    out[...] = fields[...]
    goals[...] = target[...]
    for i in range(COMP):
        rate = relaxation[i]
        table[i] = rate
        for j in range(COMP):
            table[COMP + i * COMP + j] = rate * gradient[i, j] * (1.0 / 12.0)
    at = COMP + COMP * COMP
    for i, j in PAIRS:
        for order in range(3):
            table[at] = interaction[order, i, j]
            at += 1


def coefficients(table):
    rates = [table[i] for i in range(COMP)]
    mixing = [[table[COMP + i * COMP + j] for j in range(COMP)] for i in range(COMP)]
    at = COMP + COMP * COMP
    pairs = {pair: [table[at + 3 * n + order] for order in range(3)] for n, pair in enumerate(PAIRS)}
    return rates, mixing, pairs


def mixed(start, laps, mixing):
    result = []
    for i in range(COMP):
        total = start[i]
        for j in range(COMP):
            total += mixing[i][j] * laps[j]
        result.append(total)
    return result


def pieces(values):
    rest = jnp.concatenate(values, axis=0)
    result = []
    for n in range(3):
        piece = rest.astype(jnp.bfloat16)
        result.append(piece)
        rest = rest - piece.astype(jnp.float32)
    return result


def steps(chunks, weights, scalars):
    rates, mixing, pairs = scalars
    layer, _, x = lane_parts(chunks[0][0][0].shape)
    slots = chunks[0][0][0].shape[0]
    rows = []
    for v, ahead, behind, above, below, beside in chunks:
        ends = [jnp.where(x < 4, a, b) for a, b in zip(ahead, behind)]
        layers = [jnp.where(layer == 0, a, b) for a, b in zip(above, below)]
        rows += [jnp.concatenate(p, axis=1) for p in zip(*[pieces(part) for part in (v, beside, ends, layers)])]
    sums = jnp.dot(jnp.concatenate(rows, axis=0), weights[...], preferred_element_type=jnp.float32)
    count = COMP * slots
    results = []
    for n, (v, _, _, above, below, _) in enumerate(chunks):
        near = sum(sums[(3 * n + m) * count : (3 * n + m + 1) * count] for m in range(3))
        laps = [near[c * slots : (c + 1) * slots] - (above[c] + below[c]) - 90.0 * v[c] for c in range(COMP)]
        drive = [None] * COMP
        for (i, j), (a, b, c) in pairs.items():
            gap = v[i] - v[j]
            bend = c * gap
            slope = b + bend
            energy = a + slope * gap
            cross = v[i] * v[j] * (slope + bend)
            first = v[j] * energy + cross
            second = v[i] * energy - cross
            drive[i] = first if drive[i] is None else drive[i] + first
            drive[j] = second if drive[j] is None else drive[j] + second
        results.append(mixed([v[i] - rates[i] * drive[i] for i in range(COMP)], laps, mixing))
    return results


def store(slots, ref, at, values):
    for c, value in enumerate(values):
        ref[at, c, TOP : TOP + slots, :] = value
        ref[at, c, TOP - 1 : TOP, :] = value[slots - 1 :]
        ref[at, c, TOP + slots : TOP + slots + 1, :] = value[:1]


def load(slots, ref, at, offset=0):
    return [ref[at, c, TOP + offset : TOP + offset + slots, :] for c in range(COMP)]


def move(slots, work, places, weights, scalars):
    chunks = []
    for at, above, below, beside, _ in places:
        around = [load(slots, work, n) for n in (above, below, beside)]
        chunks.append((load(slots, work, at), load(slots, work, at, 1), load(slots, work, at, -1), *around))
    for place, values in zip(places, steps(chunks, weights, scalars)):
        store(slots, work, place[-1], values)


def column(ref, start, count, stride):
    flat = ref.reshape(ref.shape[0] * ref.shape[1], LANES)
    return flat[pl.ds(start, count, stride=stride), :]


SPAN = CHUNKS + 2
BLOCK, SIDE, BLOCK_NEXT, SIDE_NEXT, FINAL, BEYOND = [n * SPAN for n in range(5)] + [4 * SPAN + 2]
ENTRIES = BEYOND + 2


def inner_kernel(cap, slots, peers, *refs):
    got, (table, weights, work, block, high, low) = refs[: peers // 2], refs[peers // 2 :]
    scalars = coefficients(table)
    _, y, _ = lane_parts((slots, LANES))
    for message, whole, joined, slot, high_slot, low_slot in entries(cap, got):
        block[slot] = message[whole : whole + ROWS, :]
        rows = message[joined : joined + ROWS, :]
        high[high_slot] = rows
        low[low_slot] = rows
    for base in range(0, FINAL, SPAN):
        for at in (base, base + SPAN - 1):
            work[at] = jnp.zeros(work.shape[1:], work.dtype)

    @pl.loop(0, CHUNKS)
    def _(k):
        rows = [k * COMP + c for c in range(COMP)]
        store(slots, work, BLOCK + 1 + k, [column(block, r, slots, ROWS) for r in rows])
        sides = [jnp.where(y < 4, column(high, r, slots, ROWS), column(low, r, slots, ROWS)) for r in rows]
        store(slots, work, SIDE + 1 + k, sides)

    @pl.loop(0, 2)
    def _(side):
        places = []
        for k in range(1, CHUNKS + 1):
            at = side * SPAN + k
            places.append((at, at + 1, at - 1, (1 - side) * SPAN + k, BLOCK_NEXT + at))
        move(slots, work, places, weights, scalars)

    second, third = BLOCK_NEXT + 2, BLOCK_NEXT + 3
    places = [
        (second, third, BLOCK_NEXT, SIDE_NEXT + 2, FINAL),
        (third, BLOCK_NEXT + SPAN - 1, second, SIDE_NEXT + 3, FINAL + 1),
    ]
    move(slots, work, places, weights, scalars)


def outer_kernel(slots, below, above, table, weights, _, out, work, middle, ends, sems):
    scalars = coefficients(table)
    mixing = scalars[1]
    pairs = slots // 2
    last = SPAN - 1
    _, y, _ = lane_parts((pairs, LANES))
    layer, _, _ = lane_parts((slots, LANES))

    def add(start, beyond, end):
        laps = [16.0 * turn(jnp.where(layer == 1 - end, b, 0.0), 64) - b for b in beyond]
        return mixed(start, laps, mixing)

    for end, ref in enumerate((below, above)):
        near, distant, side = [], [], []
        for c in range(COMP):
            near.append(column(ref, (1 - end) * COMP + c, slots, HALF))
            distant.append(column(ref, end * COMP + c, slots, HALF))
            both = column(ref, slots * HALF + c, pairs, COMP)
            side.append(jnp.concatenate([both, jnp.where(y < 4, turn(both, -16), turn(both, 16))], axis=0))
        edge = 1 + end * (CHUNKS - 1)
        store(slots, work, BLOCK + end * last, near)
        store(slots, work, BEYOND + end, distant)
        store(slots, work, SIDE + end * last, side)
        first = add(load(slots, work, BLOCK_NEXT + edge), near, end)
        store(slots, work, SIDE_NEXT + edge, add(load(slots, work, SIDE_NEXT + edge), side, end))
        store(slots, work, BLOCK_NEXT + edge, first)
        for c, value in enumerate(add(load(slots, work, FINAL + end), first, end)):
            middle[:, c, end * LANES : (end + 1) * LANES] = value

    copies = [pltpu.make_async_copy(middle, out.at[:, :, LANES : 3 * LANES], sems.at[2])]
    copies[0].start()

    @pl.loop(0, 2)
    def _(late):
        places = []
        for end in range(2):
            outside = end * last
            at = jnp.where(late == 1, BLOCK_NEXT + 1 + end * (CHUNKS - 1), BLOCK + outside)
            beyond = jnp.where(late == 1, BLOCK_NEXT + outside, BEYOND + end)
            beside = jnp.where(late == 1, SIDE_NEXT + 1 + end * (CHUNKS - 1), SIDE + outside)
            to = jnp.where(late == 1, BLOCK, BLOCK_NEXT) + outside
            up, down = (beyond, at - 1) if end else (at + 1, beyond)
            places.append((at, up, down, beside, to))
        move(slots, work, places, weights, scalars)

    for end in range(2):
        for c, value in enumerate(load(slots, work, BLOCK + end * last)):
            ends[end, :, c, :] = value
        at = end * (CHUNKS - 1) * LANES
        copies.append(pltpu.make_async_copy(ends.at[end], out.at[:, :, at : at + LANES], sems.at[end]))
        copies[-1].start()
    for copy in copies:
        copy.wait()


def per_device(fields, target, gradient_matrix, relaxation, interaction):
    slots = fields.shape[0]
    peers = lax.axis_size("loc")
    groups = lax.axis_size("grp")
    cap = (slots + peers - 1) // peers
    chips = peers // 2
    f32 = jnp.float32
    params = pltpu.CompilerParams(vmem_limit_bytes=8 << 20)

    def shape(*dims):
        return pltpu.VMEM(dims, f32)

    def inside(*arrays):
        return [pltpu.with_memory_space_constraint(a, pltpu.VMEM) for a in arrays]

    def cross(array, flip):
        return lax.ppermute(array, "loc", [(i, i ^ flip) for i in range(peers)])

    target = target.reshape(1, slots)
    staged, goals, table = pl.pallas_call(
        stage_kernel,
        out_shape=(shape(*fields.shape), pltpu.VMEM(target.shape, jnp.int32), pltpu.SMEM((TABLE,), f32)),
        in_specs=[VMEM] * 2 + [SMEM] * 3,
        out_specs=(VMEM, VMEM, SMEM),
        name="stage",
    )(fields, target, gradient_matrix, relaxation, interaction)
    table = pltpu.with_memory_space_constraint(table, pltpu.SMEM)
    other_fields, other_target = cross(fields, 1), cross(target, 1)
    entry_count = 2 * peers * cap
    routes = pl.pallas_call(
        lambda *refs: route_kernel(peers, cap, slots, *refs),
        out_shape=(pltpu.SMEM((entry_count,), jnp.int32),) * 2,
        in_specs=[VMEM] * 2,
        out_specs=(SMEM,) * 2,
        scratch_shapes=[pltpu.SMEM((2 * peers,), jnp.int32)],
        name="route",
        compiler_params=params,
    )(*inside(goals, other_target))
    routes = [pltpu.with_memory_space_constraint(a, pltpu.SMEM) for a in routes]

    def pack(flip):
        message = shape(4 * cap * ROWS + 8, LANES)
        extra = () if flip else (pltpu.VMEM((4 * LANES, LANES), jnp.bfloat16),)
        return pl.pallas_call(
            lambda *refs: pack_kernel(peers, cap, flip, *refs),
            out_shape=(message, *extra),
            in_specs=[SMEM] * 2 + [VMEM] * 2,
            out_specs=(VMEM,) * (1 + len(extra)),
            name="pack",
            compiler_params=params,
        )(*routes, *inside(staged, other_fields))

    flips = [2 * j for j in reversed(range(chips))]
    *sent, (own, weights) = [pack(flip) for flip in flips]
    weights = inside(weights)[0]
    got = inside(*[cross(message, flip) for (message,), flip in zip(sent, flips)], own)
    up, down = pl.pallas_call(
        lambda *refs: faces_kernel(cap, slots, *refs),
        out_shape=(shape(slots + slots // 4, HALF, LANES),) * 2,
        in_specs=[VMEM] * chips,
        out_specs=(VMEM,) * 2,
        scratch_shapes=[pltpu.VMEM((slots + 1, HALF, LANES), f32)] * 2,
        name="faces",
        compiler_params=params,
    )(*got)
    forward = [(i, (i + 1) % groups) for i in range(groups)]
    backward = [(j, i) for i, j in forward]
    below = lax.ppermute(up, "grp", forward)
    above = lax.ppermute(down, "grp", backward)
    work = pl.pallas_call(
        lambda *refs: inner_kernel(cap, slots, peers, *refs),
        out_shape=shape(ENTRIES, COMP, DEPTH, LANES),
        in_specs=[VMEM] * chips + [SMEM, VMEM],
        out_specs=VMEM,
        scratch_shapes=[pltpu.VMEM((slots + 1, ROWS, LANES), f32)] * 3,
        name="inner",
        compiler_params=params,
    )(*got, table, weights)
    return pl.pallas_call(
        lambda *refs: outer_kernel(slots, *refs),
        out_shape=(jax.ShapeDtypeStruct(fields.shape, f32), shape(*work.shape)),
        in_specs=[VMEM] * 2 + [SMEM] + [VMEM] * 2,
        out_specs=(pl.BlockSpec(memory_space=pl.ANY), VMEM),
        input_output_aliases={4: 1},
        scratch_shapes=[
            pltpu.VMEM((slots, COMP, 2 * LANES), f32),
            pltpu.VMEM((2, slots, COMP, LANES), f32),
            pltpu.SemaphoreType.DMA((3,)),
        ],
        name="outer",
        compiler_params=params,
    )(*inside(below, above), table, weights, *inside(work))[0]


def solution(mesh):
    placed = (P(("grp", "loc"), None, None), P(("grp", "loc")), P(), P(), P())
    return jax.shard_map(
        per_device,
        mesh=mesh,
        in_specs=placed,
        out_specs=P(("grp", "loc"), None, None),
        check_vma=False,
    )
```

```python
import jax
import jax.numpy as jnp
from jax import lax
from jax.experimental import pallas as pl
from jax.experimental.pallas import tpu as pltpu
from jax.sharding import PartitionSpec as P

COMP = 4
LANES = 128
CHUNKS = 4
ROWS = CHUNKS * COMP
HALF = ROWS // 2
TOP = 8
DEPTH = 32
PAIRS = [(i, j) for i in range(COMP) for j in range(i + 1, COMP)]
TABLE = COMP + COMP * COMP + 3 * len(PAIRS)

VMEM = pl.BlockSpec(memory_space=pltpu.VMEM)
SMEM = pl.BlockSpec(memory_space=pltpu.SMEM)


def lane_parts(shape):
    lane = lax.broadcasted_iota(jnp.int32, shape, 1)
    return lane // 64, (lane // 8) % 8, lane % 8


def turn(v, shift):
    return pltpu.roll(v, shift % LANES, 1)


def route_kernel(peers, cap, slots, target, other_target, held, label, count):
    for core, goals in enumerate((target[...], other_target[...])):
        for peer in range(peers):
            count[core * peers + peer] = 0
            for k in range(cap):
                held[(core * peers + peer) * cap + k] = 0
                label[(core * peers + peer) * cap + k] = slots
        for i in range(slots):
            goal = goals[0, i]
            peer = core * peers + lax.div(goal, slots)
            k = count[peer]
            count[peer] = k + 1
            held[peer * cap + k] = i
            label[peer * cap + k] = lax.rem(goal, slots)


def pack_kernel(peers, cap, flip, held, label, fields, other_fields, out, *weights):
    _, y, _ = lane_parts((COMP, LANES))
    row = lax.broadcasted_iota(jnp.int32, (8, LANES), 1)
    peer = lax.axis_index("loc") ^ flip
    places = [lax.rem(peer + d, peers) * cap for d in (0, 1, peers - 1)]
    names = jnp.zeros((8, LANES), jnp.int32)
    for core, source in enumerate((fields, other_fields)):
        for k in range(cap):
            own, high, low = [held[core * peers * cap + at + k] for at in places]
            entry = core * cap + k
            for n, at in enumerate(places):
                names = jnp.where(row == 2 * cap * n + entry, label[core * peers * cap + at + k], names)
            for chunk in range(CHUNKS):
                part = slice(chunk * LANES, (chunk + 1) * LANES)
                at = entry * ROWS + chunk * COMP
                out[at : at + COMP, :] = source[own, :, part]
                at += 2 * cap * ROWS
                out[at : at + COMP, :] = jnp.where(y < 4, source[high, :, part], source[low, :, part])
    out[4 * cap * ROWS :, :] = names.astype(jnp.float32)
    if weights:
        fill_weights(weights[0])


def fill_weights(out):
    shape = (LANES, LANES)
    z, y, x = lane_parts(shape)
    source = lax.broadcasted_iota(jnp.int32, shape, 0)
    dz, dy, dx = source // 64 - z, (source // 8) % 8 - y, source % 8 - x

    def stencil(d):
        return jnp.where(jnp.abs(d) == 1, 16.0, jnp.where(jnp.abs(d) == 2, -1.0, 0.0))

    def only(mask, value):
        return jnp.where(mask, value, 0.0)

    swap = only((dz != 0) & (dy == 0) & (dx == 0), 16.0)
    along_y, along_x = (dz == 0) & (dx == 0), (dz == 0) & (dy == 0)
    parts = (
        swap + only(along_y, stencil(dy)) + only(along_x, stencil(dx)),
        only(along_y, stencil(dy + 8) + stencil(dy - 8)),
        only(along_x, stencil(dx + 8) + stencil(dx - 8)),
        swap,
    )
    for n, part in enumerate(parts):
        out[n * LANES : (n + 1) * LANES, :] = part.astype(out.dtype)


def entries(cap, got):
    for message in got:
        names = message[4 * cap * ROWS : 4 * cap * ROWS + 1, :].astype(jnp.int32)
        for k in range(2 * cap):
            yield message, k * ROWS, (2 * cap + k) * ROWS, names[0, k], names[0, 2 * cap + k], names[0, 4 * cap + k]


def squeeze(one, two, y):
    return jnp.where((y >= 2) & (y < 6), jnp.where(y < 4, turn(two, 16), turn(two, -16)), one)


def second_of(both, y):
    return jnp.where(y < 4, turn(both, -16), turn(both, 16))


def bundle_rows(cap, count):
    corners = 2 * cap * count * HALF
    names = corners + cap * count * COMP
    return corners, names, names + 8 * ((count + 7) // 8)


def bundle(cap, got, out):
    corners, names, end = bundle_rows(cap, len(got))
    _, y, _ = lane_parts((COMP, LANES))
    out[names:, :] = jnp.zeros((end - names, LANES), out.dtype)
    for n, message in enumerate(got):
        for k in range(2 * cap):
            at = (2 * cap * n + k) * HALF
            out[at : at + HALF, :] = message[k * ROWS + HALF : (k + 1) * ROWS, :]
        for k in range(cap):
            one, two = [message[(2 * cap + e + 1) * ROWS - COMP : (2 * cap + e + 1) * ROWS, :] for e in (k, cap + k)]
            at = corners + (cap * n + k) * COMP
            out[at : at + COMP, :] = squeeze(one, two, y)
        out[names + n : names + n + 1, :] = message[4 * cap * ROWS : 4 * cap * ROWS + 1, :]


def put_down(cap, got, down, high, low):
    for message, whole, joined, slot, high_slot, low_slot in entries(cap, got):
        down[slot] = message[whole : whole + HALF, :]
        rows = message[joined : joined + COMP, :]
        high[high_slot] = rows
        low[low_slot] = rows


def put_sides(slots, faces, high, low):
    _, y, _ = lane_parts((COMP, LANES))
    pairs = slots // 2
    for q in range(pairs):
        one, two = [jnp.where(y < 4, high[t], low[t]) for t in (q, q + pairs)]
        at = (q % 2) * COMP
        faces[slots + q // 2, at : at + COMP, :] = squeeze(one, two, y)


def early_kernel(cap, *refs):
    got, (up, down, high, low) = refs[:-4], refs[-4:]
    bundle(cap, got, up)
    put_down(cap, got, down, high, low)


def late_kernel(cap, slots, count, *refs):
    got, (up, down, high, low) = refs[:count], refs[-4:]
    bundle(cap, got, up)
    put_down(cap, got, down, high, low)
    put_sides(slots, down, high, low)


def catch_kernel(cap, slots, counts, *refs):
    joined, faces, high, low = refs
    split = bundle_rows(cap, counts[0])[-1]
    refs = joined.at[:split], joined.at[split:]
    _, y, _ = lane_parts((COMP, LANES))
    for ref, count in zip(refs, counts):
        corners, names, _ = bundle_rows(cap, count)
        for n in range(count):
            slot_of = ref[names + n : names + n + 1, :].astype(jnp.int32)
            for k in range(2 * cap):
                at = (2 * cap * n + k) * HALF
                faces[slot_of[0, k]] = ref[at : at + HALF, :]
                at = corners + (cap * n + k % cap) * COMP
                rows = ref[at : at + COMP, :]
                if k >= cap:
                    rows = second_of(rows, y)
                high[slot_of[0, 2 * cap + k]] = rows
                low[slot_of[0, 4 * cap + k]] = rows
    put_sides(slots, faces, high, low)


def stage_kernel(fields, target, gradient, relaxation, interaction, out, goals, table):
    out[...] = fields[...]
    goals[...] = target[...]
    for i in range(COMP):
        rate = relaxation[i]
        table[i] = rate
        for j in range(COMP):
            table[COMP + i * COMP + j] = rate * gradient[i, j] * (1.0 / 12.0)
    at = COMP + COMP * COMP
    for i, j in PAIRS:
        for order in range(3):
            table[at] = interaction[order, i, j]
            at += 1


def coefficients(table):
    rates = [table[i] for i in range(COMP)]
    mixing = [[table[COMP + i * COMP + j] for j in range(COMP)] for i in range(COMP)]
    at = COMP + COMP * COMP
    pairs = {pair: [table[at + 3 * n + order] for order in range(3)] for n, pair in enumerate(PAIRS)}
    return rates, mixing, pairs


def mixed(start, laps, mixing):
    result = []
    for i in range(COMP):
        total = start[i]
        for j in range(COMP):
            total += mixing[i][j] * laps[j]
        result.append(total)
    return result


def pieces(values):
    rest = jnp.concatenate(values, axis=0)
    result = []
    for n in range(3):
        piece = rest.astype(jnp.bfloat16)
        result.append(piece)
        rest = rest - piece.astype(jnp.float32)
    return result


def steps(chunks, weights, scalars):
    rates, mixing, pairs = scalars
    layer, _, x = lane_parts(chunks[0][0][0].shape)
    slots = chunks[0][0][0].shape[0]
    rows = []
    for v, ahead, behind, above, below, beside in chunks:
        ends = [jnp.where(x < 4, a, b) for a, b in zip(ahead, behind)]
        layers = [jnp.where(layer == 0, a, b) for a, b in zip(above, below)]
        rows += [jnp.concatenate(p, axis=1) for p in zip(*[pieces(part) for part in (v, beside, ends, layers)])]
    sums = jnp.dot(jnp.concatenate(rows, axis=0), weights[...], preferred_element_type=jnp.float32)
    count = COMP * slots
    results = []
    for n, (v, _, _, above, below, _) in enumerate(chunks):
        near = sum(sums[(3 * n + m) * count : (3 * n + m + 1) * count] for m in range(3))
        laps = [near[c * slots : (c + 1) * slots] - (above[c] + below[c]) - 90.0 * v[c] for c in range(COMP)]
        drive = [None] * COMP
        for (i, j), (a, b, c) in pairs.items():
            gap = v[i] - v[j]
            bend = c * gap
            slope = b + bend
            energy = a + slope * gap
            cross = v[i] * v[j] * (slope + bend)
            first = v[j] * energy + cross
            second = v[i] * energy - cross
            drive[i] = first if drive[i] is None else drive[i] + first
            drive[j] = second if drive[j] is None else drive[j] + second
        results.append(mixed([v[i] - rates[i] * drive[i] for i in range(COMP)], laps, mixing))
    return results


def store(slots, ref, at, values):
    for c, value in enumerate(values):
        ref[at, c, TOP : TOP + slots, :] = value
        ref[at, c, TOP - 1 : TOP, :] = value[slots - 1 :]
        ref[at, c, TOP + slots : TOP + slots + 1, :] = value[:1]


def load(slots, ref, at, offset=0):
    return [ref[at, c, TOP + offset : TOP + offset + slots, :] for c in range(COMP)]


def move(slots, work, places, weights, scalars):
    chunks = []
    for at, above, below, beside, _ in places:
        around = [load(slots, work, n) for n in (above, below, beside)]
        chunks.append((load(slots, work, at), load(slots, work, at, 1), load(slots, work, at, -1), *around))
    for place, values in zip(places, steps(chunks, weights, scalars)):
        store(slots, work, place[-1], values)


def column(ref, start, count, stride):
    flat = ref.reshape(ref.shape[0] * ref.shape[1], LANES)
    return flat[pl.ds(start, count, stride=stride), :]


SPAN = CHUNKS + 2
BLOCK, SIDE, BLOCK_NEXT, SIDE_NEXT, FINAL, BEYOND = [n * SPAN for n in range(5)] + [4 * SPAN + 2]
ENTRIES = BEYOND + 2


def inner_kernel(cap, slots, peers, *refs):
    got, (table, weights, work, block, high, low) = refs[: peers // 2], refs[peers // 2 :]
    scalars = coefficients(table)
    _, y, _ = lane_parts((slots, LANES))
    for message, whole, joined, slot, high_slot, low_slot in entries(cap, got):
        block[slot] = message[whole : whole + ROWS, :]
        rows = message[joined : joined + ROWS, :]
        high[high_slot] = rows
        low[low_slot] = rows
    for base in range(0, FINAL, SPAN):
        for at in (base, base + SPAN - 1):
            work[at] = jnp.zeros(work.shape[1:], work.dtype)

    @pl.loop(0, CHUNKS)
    def _(k):
        rows = [k * COMP + c for c in range(COMP)]
        store(slots, work, BLOCK + 1 + k, [column(block, r, slots, ROWS) for r in rows])
        sides = [jnp.where(y < 4, column(high, r, slots, ROWS), column(low, r, slots, ROWS)) for r in rows]
        store(slots, work, SIDE + 1 + k, sides)

    @pl.loop(0, 2)
    def _(side):
        places = []
        for k in range(1, CHUNKS + 1):
            at = side * SPAN + k
            places.append((at, at + 1, at - 1, (1 - side) * SPAN + k, BLOCK_NEXT + at))
        move(slots, work, places, weights, scalars)

    second, third = BLOCK_NEXT + 2, BLOCK_NEXT + 3
    places = [
        (second, third, BLOCK_NEXT, SIDE_NEXT + 2, FINAL),
        (third, BLOCK_NEXT + SPAN - 1, second, SIDE_NEXT + 3, FINAL + 1),
    ]
    move(slots, work, places, weights, scalars)


def outer_kernel(slots, below, above, table, weights, _, out, work, middle, ends, sems):
    scalars = coefficients(table)
    mixing = scalars[1]
    pairs = slots // 2
    last = SPAN - 1
    _, y, _ = lane_parts((pairs, LANES))
    layer, _, _ = lane_parts((slots, LANES))

    def add(start, beyond, end):
        laps = [16.0 * turn(jnp.where(layer == 1 - end, b, 0.0), 64) - b for b in beyond]
        return mixed(start, laps, mixing)

    for end, ref in enumerate((below, above)):
        near, distant, side = [], [], []
        for c in range(COMP):
            near.append(column(ref, (1 - end) * COMP + c, slots, HALF))
            distant.append(column(ref, end * COMP + c, slots, HALF))
            both = column(ref, slots * HALF + c, pairs, COMP)
            side.append(jnp.concatenate([both, second_of(both, y)], axis=0))
        edge = 1 + end * (CHUNKS - 1)
        store(slots, work, BLOCK + end * last, near)
        store(slots, work, BEYOND + end, distant)
        store(slots, work, SIDE + end * last, side)
        first = add(load(slots, work, BLOCK_NEXT + edge), near, end)
        store(slots, work, SIDE_NEXT + edge, add(load(slots, work, SIDE_NEXT + edge), side, end))
        store(slots, work, BLOCK_NEXT + edge, first)
        for c, value in enumerate(add(load(slots, work, FINAL + end), first, end)):
            middle[:, c, end * LANES : (end + 1) * LANES] = value

    copies = [pltpu.make_async_copy(middle, out.at[:, :, LANES : 3 * LANES], sems.at[2])]
    copies[0].start()

    @pl.loop(0, 2)
    def _(late):
        places = []
        for end in range(2):
            outside = end * last
            at = jnp.where(late == 1, BLOCK_NEXT + 1 + end * (CHUNKS - 1), BLOCK + outside)
            beyond = jnp.where(late == 1, BLOCK_NEXT + outside, BEYOND + end)
            beside = jnp.where(late == 1, SIDE_NEXT + 1 + end * (CHUNKS - 1), SIDE + outside)
            to = jnp.where(late == 1, BLOCK, BLOCK_NEXT) + outside
            up, down = (beyond, at - 1) if end else (at + 1, beyond)
            places.append((at, up, down, beside, to))
        move(slots, work, places, weights, scalars)

    for end in range(2):
        for c, value in enumerate(load(slots, work, BLOCK + end * last)):
            ends[end, :, c, :] = value
        at = end * (CHUNKS - 1) * LANES
        copies.append(pltpu.make_async_copy(ends.at[end], out.at[:, :, at : at + LANES], sems.at[end]))
        copies[-1].start()
    for copy in copies:
        copy.wait()


def per_device(fields, target, gradient_matrix, relaxation, interaction):
    slots = fields.shape[0]
    peers = lax.axis_size("loc")
    groups = lax.axis_size("grp")
    cap = (slots + peers - 1) // peers
    chips = peers // 2
    f32 = jnp.float32
    params = pltpu.CompilerParams(vmem_limit_bytes=8 << 20)

    def shape(*dims):
        return pltpu.VMEM(dims, f32)

    def inside(*arrays):
        return [pltpu.with_memory_space_constraint(a, pltpu.VMEM) for a in arrays]

    def cross(array, flip):
        return lax.ppermute(array, "loc", [(i, i ^ flip) for i in range(peers)])

    target = target.reshape(1, slots)
    staged, goals, table = pl.pallas_call(
        stage_kernel,
        out_shape=(shape(*fields.shape), pltpu.VMEM(target.shape, jnp.int32), pltpu.SMEM((TABLE,), f32)),
        in_specs=[VMEM] * 2 + [SMEM] * 3,
        out_specs=(VMEM, VMEM, SMEM),
        name="stage",
    )(fields, target, gradient_matrix, relaxation, interaction)
    table = pltpu.with_memory_space_constraint(table, pltpu.SMEM)
    other_fields, other_target = cross(fields, 1), cross(target, 1)
    entry_count = 2 * peers * cap
    routes = pl.pallas_call(
        lambda *refs: route_kernel(peers, cap, slots, *refs),
        out_shape=(pltpu.SMEM((entry_count,), jnp.int32),) * 2,
        in_specs=[VMEM] * 2,
        out_specs=(SMEM,) * 2,
        scratch_shapes=[pltpu.SMEM((2 * peers,), jnp.int32)],
        name="route",
        compiler_params=params,
    )(*inside(goals, other_target))
    routes = [pltpu.with_memory_space_constraint(a, pltpu.SMEM) for a in routes]

    def pack(flip):
        message = shape(4 * cap * ROWS + 8, LANES)
        extra = () if flip else (pltpu.VMEM((4 * LANES, LANES), jnp.bfloat16),)
        return pl.pallas_call(
            lambda *refs: pack_kernel(peers, cap, flip, *refs),
            out_shape=(message, *extra),
            in_specs=[SMEM] * 2 + [VMEM] * 2,
            out_specs=(VMEM,) * (1 + len(extra)),
            name="pack",
            compiler_params=params,
        )(*routes, *inside(staged, other_fields))

    flips = [2 * j for j in reversed(range(chips))]
    *sent, (own, weights) = [pack(flip) for flip in flips]
    weights = inside(weights)[0]
    got = inside(*[cross(message, flip) for (message,), flip in zip(sent, flips)], own)
    early, late = got[: chips // 2 - 1] + got[-1:], got[chips // 2 - 1 : -1]
    counts = len(early), len(late)
    face, corner = (slots + slots // 4, HALF, LANES), (slots + 1, COMP, LANES)
    up_early, *down = pl.pallas_call(
        lambda *refs: early_kernel(cap, *refs),
        out_shape=(shape(bundle_rows(cap, counts[0])[-1], LANES), shape(*face), shape(*corner), shape(*corner)),
        in_specs=[VMEM] * counts[0],
        out_specs=(VMEM,) * 4,
        name="early",
        compiler_params=params,
    )(*early)
    up_late, down, *_ = pl.pallas_call(
        lambda *refs: late_kernel(cap, slots, counts[1], *refs),
        out_shape=(shape(bundle_rows(cap, counts[1])[-1], LANES), shape(*face), shape(*corner), shape(*corner)),
        in_specs=[VMEM] * (counts[1] + 3),
        out_specs=(VMEM,) * 4,
        input_output_aliases={counts[1] + n: 1 + n for n in range(3)},
        name="late",
        compiler_params=params,
    )(*late, *inside(*down))
    forward = [(i, (i + 1) % groups) for i in range(groups)]
    backward = [(j, i) for i, j in forward]
    from_below = [lax.ppermute(up, "grp", forward) for up in (up_early, up_late)]
    above = lax.ppermute(down, "grp", backward)
    below = pl.pallas_call(
        lambda *refs: catch_kernel(cap, slots, counts, *refs),
        out_shape=shape(*face),
        in_specs=[VMEM],
        out_specs=VMEM,
        scratch_shapes=[pltpu.VMEM(corner, f32)] * 2,
        name="catch",
        compiler_params=params,
    )(*inside(jnp.concatenate(from_below)))
    work = pl.pallas_call(
        lambda *refs: inner_kernel(cap, slots, peers, *refs),
        out_shape=shape(ENTRIES, COMP, DEPTH, LANES),
        in_specs=[VMEM] * chips + [SMEM, VMEM],
        out_specs=VMEM,
        scratch_shapes=[pltpu.VMEM((slots + 1, ROWS, LANES), f32)] * 3,
        name="inner",
        compiler_params=params,
    )(*got, table, weights)
    return pl.pallas_call(
        lambda *refs: outer_kernel(slots, *refs),
        out_shape=(jax.ShapeDtypeStruct(fields.shape, f32), shape(*work.shape)),
        in_specs=[VMEM] * 2 + [SMEM] + [VMEM] * 2,
        out_specs=(pl.BlockSpec(memory_space=pl.ANY), VMEM),
        input_output_aliases={4: 1},
        scratch_shapes=[
            pltpu.VMEM((slots, COMP, 2 * LANES), f32),
            pltpu.VMEM((2, slots, COMP, LANES), f32),
            pltpu.SemaphoreType.DMA((3,)),
        ],
        name="outer",
        compiler_params=params,
    )(*inside(below, above), table, weights, *inside(work))[0]


def solution(mesh):
    placed = (P(("grp", "loc"), None, None), P(("grp", "loc")), P(), P(), P())
    return jax.shard_map(
        per_device,
        mesh=mesh,
        in_specs=placed,
        out_specs=P(("grp", "loc"), None, None),
        check_vma=False,
    )
```

```python
import jax
import jax.numpy as jnp
from jax import lax
from jax.experimental import pallas as pl
from jax.experimental.pallas import tpu as pltpu
from jax.sharding import PartitionSpec as P

COMP = 4
LANES = 128
CHUNKS = 4
ROWS = CHUNKS * COMP
HALF = ROWS // 2
TOP = 8
DEPTH = 32
PAIRS = [(i, j) for i in range(COMP) for j in range(i + 1, COMP)]
TABLE = COMP + COMP * COMP + 3 * len(PAIRS)

VMEM = pl.BlockSpec(memory_space=pltpu.VMEM)
SMEM = pl.BlockSpec(memory_space=pltpu.SMEM)


def lane_parts(shape):
    lane = lax.broadcasted_iota(jnp.int32, shape, 1)
    return lane // 64, (lane // 8) % 8, lane % 8


def turn(v, shift):
    return pltpu.roll(v, shift % LANES, 1)


def route(peers, cap, slots, goal_of, held, label, count):
    for peer in range(peers):
        count[peer] = 0
        for k in range(cap):
            held[peer * cap + k] = 0
            label[peer * cap + k] = slots
    for i in range(slots):
        goal = goal_of(i)
        peer = lax.div(goal, slots)
        k = count[peer]
        count[peer] = k + 1
        held[peer * cap + k] = i
        label[peer * cap + k] = lax.rem(goal, slots)


def other_route_kernel(peers, cap, slots, target, held, label, count):
    goals = target[...]
    route(peers, cap, slots, lambda i: goals[0, i], held, label, count)


def pack_kernel(peers, cap, flip, held, label, other_held, other_label, fields, other_fields, out, *weights):
    _, y, _ = lane_parts((COMP, LANES))
    row = lax.broadcasted_iota(jnp.int32, (8, LANES), 1)
    peer = lax.axis_index("loc") ^ flip
    places = [lax.rem(peer + d, peers) * cap for d in (0, 1, peers - 1)]
    names = jnp.zeros((8, LANES), jnp.int32)
    for core, (source, held, label) in enumerate(((fields, held, label), (other_fields, other_held, other_label))):
        for k in range(cap):
            own, high, low = [held[at + k] for at in places]
            entry = core * cap + k
            for n, at in enumerate(places):
                names = jnp.where(row == 2 * cap * n + entry, label[at + k], names)
            for chunk in range(CHUNKS):
                part = slice(chunk * LANES, (chunk + 1) * LANES)
                at = entry * ROWS + chunk * COMP
                out[at : at + COMP, :] = source[own, :, part]
                at += 2 * cap * ROWS
                out[at : at + COMP, :] = jnp.where(y < 4, source[high, :, part], source[low, :, part])
    out[4 * cap * ROWS :, :] = names.astype(jnp.float32)
    if weights:
        fill_weights(weights[0])


def fill_weights(out):
    shape = (LANES, LANES)
    z, y, x = lane_parts(shape)
    source = lax.broadcasted_iota(jnp.int32, shape, 0)
    dz, dy, dx = source // 64 - z, (source // 8) % 8 - y, source % 8 - x

    def stencil(d):
        return jnp.where(jnp.abs(d) == 1, 16.0, jnp.where(jnp.abs(d) == 2, -1.0, 0.0))

    def only(mask, value):
        return jnp.where(mask, value, 0.0)

    swap = only((dz != 0) & (dy == 0) & (dx == 0), 16.0)
    along_y, along_x = (dz == 0) & (dx == 0), (dz == 0) & (dy == 0)
    parts = (
        swap + only(along_y, stencil(dy)) + only(along_x, stencil(dx)),
        only(along_y, stencil(dy + 8) + stencil(dy - 8)),
        only(along_x, stencil(dx + 8) + stencil(dx - 8)),
        swap,
    )
    for n, part in enumerate(parts):
        out[n * LANES : (n + 1) * LANES, :] = part.astype(out.dtype)


def entries(cap, got):
    for message in got:
        names = message[4 * cap * ROWS : 4 * cap * ROWS + 1, :].astype(jnp.int32)
        for k in range(2 * cap):
            yield message, k * ROWS, (2 * cap + k) * ROWS, names[0, k], names[0, 2 * cap + k], names[0, 4 * cap + k]


def squeeze(one, two, y):
    return jnp.where((y >= 2) & (y < 6), jnp.where(y < 4, turn(two, 16), turn(two, -16)), one)


def second_of(both, y):
    return jnp.where(y < 4, turn(both, -16), turn(both, 16))


def bundle_rows(cap, count):
    corners = 2 * cap * count * HALF
    names = corners + cap * count * COMP
    return corners, names, names + 8 * ((count + 7) // 8)


def bundle(cap, count, got, out, before=0):
    corners, names, end = bundle_rows(cap, count)
    _, y, _ = lane_parts((COMP, LANES))
    if before == 0:
        out[names:, :] = jnp.zeros((end - names, LANES), out.dtype)
    for n, message in enumerate(got, before):
        for k in range(2 * cap):
            at = (2 * cap * n + k) * HALF
            out[at : at + HALF, :] = message[k * ROWS + HALF : (k + 1) * ROWS, :]
        for k in range(cap):
            one, two = [message[(2 * cap + e + 1) * ROWS - COMP : (2 * cap + e + 1) * ROWS, :] for e in (k, cap + k)]
            at = corners + (cap * n + k) * COMP
            out[at : at + COMP, :] = squeeze(one, two, y)
        out[names + n : names + n + 1, :] = message[4 * cap * ROWS : 4 * cap * ROWS + 1, :]


def put_down(cap, got, down, high, low):
    for message, whole, joined, slot, high_slot, low_slot in entries(cap, got):
        down[slot] = message[whole : whole + HALF, :]
        put_corner(message[joined : joined + COMP, :], high, high_slot, low, low_slot)


def put_corner(rows, high, high_slot, low, low_slot):
    high[pl.ds(pl.multiple_of(high_slot * COMP, COMP), COMP), :] = rows
    low[pl.ds(pl.multiple_of(low_slot * COMP, COMP), COMP), :] = rows


def put_sides(slots, faces, high, low):
    half = slots // 2 * COMP
    _, y, _ = lane_parts((half, LANES))
    one, two = [jnp.where(y < 4, high[at : at + half, :], low[at : at + half, :]) for at in (0, half)]
    both = squeeze(one, two, y)
    for n in range(half // HALF):
        faces[slots + n] = both[n * HALF : (n + 1) * HALF]


def early_kernel(cap, count, *refs):
    got, (up, down, high, low) = refs[:-4], refs[-4:]
    bundle(cap, count, got, up)
    put_down(cap, got, down, high, low)


def next_kernel(cap, *refs):
    got, (up, down, high, low) = refs[:-7], refs[-4:]
    bundle(cap, len(got) + 1, got, up)
    put_down(cap, got, down, high, low)


def last_kernel(cap, slots, count, message, *refs):
    up, down, high, low = refs[-4:]
    bundle(cap, count, [message], up, count - 1)
    put_down(cap, [message], down, high, low)
    put_sides(slots, down, high, low)


def catch_kernel(cap, slots, counts, *refs):
    joined, faces, high, low = refs
    split = bundle_rows(cap, counts[0])[-1]
    refs = joined.at[:split], joined.at[split:]
    _, y, _ = lane_parts((COMP, LANES))
    for ref, count in zip(refs, counts):
        corners, names, _ = bundle_rows(cap, count)
        for n in range(count):
            slot_of = ref[names + n : names + n + 1, :].astype(jnp.int32)
            for k in range(2 * cap):
                at = (2 * cap * n + k) * HALF
                faces[slot_of[0, k]] = ref[at : at + HALF, :]
                at = corners + (cap * n + k % cap) * COMP
                rows = ref[at : at + COMP, :]
                if k >= cap:
                    rows = second_of(rows, y)
                put_corner(rows, high, slot_of[0, 2 * cap + k], low, slot_of[0, 4 * cap + k])
    put_sides(slots, faces, high, low)


def stage_kernel(peers, cap, slots, *refs):
    arguments, (out, held, label, table), inside, (count, sems) = refs[:5], refs[5:9], refs[9:13], refs[13:]
    copies = [pltpu.make_async_copy(a, b, sems.at[n]) for n, (a, b) in enumerate(zip(arguments, (out, *inside)))]
    for copy in copies[1:] + copies[:1]:
        copy.start()
    for copy in copies[1:]:
        copy.wait()
    target, gradient, relaxation, interaction = inside
    route(peers, cap, slots, lambda i: target[i], held, label, count)
    for i in range(COMP):
        rate = relaxation[i]
        table[i] = rate
        for j in range(COMP):
            table[COMP + i * COMP + j] = rate * gradient[i, j] * (1.0 / 12.0)
    at = COMP + COMP * COMP
    for i, j in PAIRS:
        for order in range(3):
            table[at] = interaction[order, i, j]
            at += 1
    copies[0].wait()


def coefficients(table):
    rates = [table[i] for i in range(COMP)]
    mixing = [[table[COMP + i * COMP + j] for j in range(COMP)] for i in range(COMP)]
    at = COMP + COMP * COMP
    pairs = {pair: [table[at + 3 * n + order] for order in range(3)] for n, pair in enumerate(PAIRS)}
    return rates, mixing, pairs


def mixed(start, laps, mixing):
    result = []
    for i in range(COMP):
        total = start[i]
        for j in range(COMP):
            total += mixing[i][j] * laps[j]
        result.append(total)
    return result


def pieces(values):
    rest = jnp.concatenate(values, axis=0)
    result = []
    for n in range(3):
        piece = rest.astype(jnp.bfloat16)
        result.append(piece)
        rest = rest - piece.astype(jnp.float32)
    return result


def steps(chunks, weights, scalars):
    rates, mixing, pairs = scalars
    layer, _, x = lane_parts(chunks[0][0][0].shape)
    slots = chunks[0][0][0].shape[0]
    rows = []
    for v, ahead, behind, above, below, beside in chunks:
        ends = [jnp.where(x < 4, a, b) for a, b in zip(ahead, behind)]
        layers = [jnp.where(layer == 0, a, b) for a, b in zip(above, below)]
        rows += [jnp.concatenate(p, axis=1) for p in zip(*[pieces(part) for part in (v, beside, ends, layers)])]
    sums = jnp.dot(jnp.concatenate(rows, axis=0), weights[...], preferred_element_type=jnp.float32)
    count = COMP * slots
    results = []
    for n, (v, _, _, above, below, _) in enumerate(chunks):
        near = sum(sums[(3 * n + m) * count : (3 * n + m + 1) * count] for m in range(3))
        laps = [near[c * slots : (c + 1) * slots] - (above[c] + below[c]) - 90.0 * v[c] for c in range(COMP)]
        drive = [None] * COMP
        for (i, j), (a, b, c) in pairs.items():
            gap = v[i] - v[j]
            bend = c * gap
            slope = b + bend
            energy = a + slope * gap
            cross = v[i] * v[j] * (slope + bend)
            first = v[j] * energy + cross
            second = v[i] * energy - cross
            drive[i] = first if drive[i] is None else drive[i] + first
            drive[j] = second if drive[j] is None else drive[j] + second
        results.append(mixed([v[i] - rates[i] * drive[i] for i in range(COMP)], laps, mixing))
    return results


def store(slots, ref, at, values):
    for c, value in enumerate(values):
        ref[at, c, TOP : TOP + slots, :] = value
        ref[at, c, TOP - 1 : TOP, :] = value[slots - 1 :]
        ref[at, c, TOP + slots : TOP + slots + 1, :] = value[:1]


def load(slots, ref, at, offset=0):
    return [ref[at, c, TOP + offset : TOP + offset + slots, :] for c in range(COMP)]


def move(slots, work, places, weights, scalars):
    chunks = []
    for at, above, below, beside, _ in places:
        around = [load(slots, work, n) for n in (above, below, beside)]
        chunks.append((load(slots, work, at), load(slots, work, at, 1), load(slots, work, at, -1), *around))
    for place, values in zip(places, steps(chunks, weights, scalars)):
        store(slots, work, place[-1], values)


def column(ref, start, count, stride):
    flat = ref.reshape(ref.shape[0] * ref.shape[1], LANES)
    return flat[pl.ds(start, count, stride=stride), :]


SPAN = CHUNKS + 2
BLOCK, SIDE, BLOCK_NEXT, SIDE_NEXT, FINAL, BEYOND = [n * SPAN for n in range(5)] + [4 * SPAN + 2]
ENTRIES = BEYOND + 2


def inner_kernel(cap, slots, peers, *refs):
    got, (table, weights, work, block, high, low) = refs[: peers // 2], refs[peers // 2 :]
    scalars = coefficients(table)
    _, y, _ = lane_parts((slots, LANES))
    for message, whole, joined, slot, high_slot, low_slot in entries(cap, got):
        block[slot] = message[whole : whole + ROWS, :]
        rows = message[joined : joined + ROWS, :]
        high[high_slot] = rows
        low[low_slot] = rows
    for base in range(0, FINAL, SPAN):
        for at in (base, base + SPAN - 1):
            work[at] = jnp.zeros(work.shape[1:], work.dtype)

    @pl.loop(0, CHUNKS)
    def _(k):
        rows = [k * COMP + c for c in range(COMP)]
        store(slots, work, BLOCK + 1 + k, [column(block, r, slots, ROWS) for r in rows])
        sides = [jnp.where(y < 4, column(high, r, slots, ROWS), column(low, r, slots, ROWS)) for r in rows]
        store(slots, work, SIDE + 1 + k, sides)

    @pl.loop(0, 2)
    def _(side):
        places = []
        for k in range(1, CHUNKS + 1):
            at = side * SPAN + k
            places.append((at, at + 1, at - 1, (1 - side) * SPAN + k, BLOCK_NEXT + at))
        move(slots, work, places, weights, scalars)

    second, third = BLOCK_NEXT + 2, BLOCK_NEXT + 3
    places = [
        (second, third, BLOCK_NEXT, SIDE_NEXT + 2, FINAL),
        (third, BLOCK_NEXT + SPAN - 1, second, SIDE_NEXT + 3, FINAL + 1),
    ]
    move(slots, work, places, weights, scalars)


def outer_kernel(slots, below, above, table, weights, _, out, work, middle, ends, sems):
    scalars = coefficients(table)
    mixing = scalars[1]
    pairs = slots // 2
    last = SPAN - 1
    _, y, _ = lane_parts((pairs, LANES))
    layer, _, _ = lane_parts((slots, LANES))

    def add(start, beyond, end):
        laps = [16.0 * turn(jnp.where(layer == 1 - end, b, 0.0), 64) - b for b in beyond]
        return mixed(start, laps, mixing)

    for end, ref in enumerate((below, above)):
        near, distant, side = [], [], []
        for c in range(COMP):
            near.append(column(ref, (1 - end) * COMP + c, slots, HALF))
            distant.append(column(ref, end * COMP + c, slots, HALF))
            both = column(ref, slots * HALF + c, pairs, COMP)
            side.append(jnp.concatenate([both, second_of(both, y)], axis=0))
        edge = 1 + end * (CHUNKS - 1)
        store(slots, work, BLOCK + end * last, near)
        store(slots, work, BEYOND + end, distant)
        store(slots, work, SIDE + end * last, side)
        first = add(load(slots, work, BLOCK_NEXT + edge), near, end)
        store(slots, work, SIDE_NEXT + edge, add(load(slots, work, SIDE_NEXT + edge), side, end))
        store(slots, work, BLOCK_NEXT + edge, first)
        for c, value in enumerate(add(load(slots, work, FINAL + end), first, end)):
            middle[:, c, end * LANES : (end + 1) * LANES] = value

    copies = [pltpu.make_async_copy(middle, out.at[:, :, LANES : 3 * LANES], sems.at[2])]
    copies[0].start()

    @pl.loop(0, 2)
    def _(late):
        places = []
        for end in range(2):
            outside = end * last
            at = jnp.where(late == 1, BLOCK_NEXT + 1 + end * (CHUNKS - 1), BLOCK + outside)
            beyond = jnp.where(late == 1, BLOCK_NEXT + outside, BEYOND + end)
            beside = jnp.where(late == 1, SIDE_NEXT + 1 + end * (CHUNKS - 1), SIDE + outside)
            to = jnp.where(late == 1, BLOCK, BLOCK_NEXT) + outside
            up, down = (beyond, at - 1) if end else (at + 1, beyond)
            places.append((at, up, down, beside, to))
        move(slots, work, places, weights, scalars)

    for end in range(2):
        for c, value in enumerate(load(slots, work, BLOCK + end * last)):
            ends[end, :, c, :] = value
        at = end * (CHUNKS - 1) * LANES
        copies.append(pltpu.make_async_copy(ends.at[end], out.at[:, :, at : at + LANES], sems.at[end]))
        copies[-1].start()
    for copy in copies:
        copy.wait()


def per_device(fields, target, gradient_matrix, relaxation, interaction):
    slots = fields.shape[0]
    peers = lax.axis_size("loc")
    groups = lax.axis_size("grp")
    cap = (slots + peers - 1) // peers
    chips = peers // 2
    f32 = jnp.float32
    params = pltpu.CompilerParams(vmem_limit_bytes=8 << 20)

    def shape(*dims):
        return pltpu.VMEM(dims, f32)

    def inside(*arrays):
        return [pltpu.with_memory_space_constraint(a, pltpu.VMEM) for a in arrays]

    def cross(array, flip):
        return lax.ppermute(array, "loc", [(i, i ^ flip) for i in range(peers)])

    numbers = pltpu.SMEM((peers * cap,), jnp.int32)
    arguments = fields, target, gradient_matrix, relaxation, interaction
    staged, held, label, table = pl.pallas_call(
        lambda *refs: stage_kernel(peers, cap, slots, *refs),
        out_shape=(shape(*fields.shape), numbers, numbers, pltpu.SMEM((TABLE,), f32)),
        in_specs=[pl.BlockSpec(memory_space=pl.ANY)] * 5,
        out_specs=(VMEM, SMEM, SMEM, SMEM),
        scratch_shapes=[pltpu.SMEM(a.shape, a.dtype) for a in arguments[1:]]
        + [pltpu.SMEM((peers,), jnp.int32), pltpu.SemaphoreType.DMA((5,))],
        name="stage",
    )(*arguments)
    table = pltpu.with_memory_space_constraint(table, pltpu.SMEM)
    other_fields, other_target = cross(fields, 1), cross(target.reshape(1, slots), 1)
    other = pl.pallas_call(
        lambda *refs: other_route_kernel(peers, cap, slots, *refs),
        out_shape=(numbers, numbers),
        in_specs=[VMEM],
        out_specs=(SMEM,) * 2,
        scratch_shapes=[pltpu.SMEM((peers,), jnp.int32)],
        name="route",
        compiler_params=params,
    )(*inside(other_target))
    routes = [pltpu.with_memory_space_constraint(a, pltpu.SMEM) for a in (held, label, *other)]

    def pack(flip):
        message = shape(4 * cap * ROWS + 8, LANES)
        extra = () if flip else (pltpu.VMEM((4 * LANES, LANES), jnp.bfloat16),)
        return pl.pallas_call(
            lambda *refs: pack_kernel(peers, cap, flip, *refs),
            out_shape=(message, *extra),
            in_specs=[SMEM] * 4 + [VMEM] * 2,
            out_specs=(VMEM,) * (1 + len(extra)),
            name="pack",
            compiler_params=params,
        )(*routes, *inside(staged, other_fields))

    flips = [2 * j for j in reversed(range(chips))]
    *sent, (own, weights) = [pack(flip) for flip in flips]
    weights = inside(weights)[0]
    got = inside(*[cross(message, flip) for (message,), flip in zip(sent, flips)], own)
    early, late = got[: chips // 2 - 1] + got[-1:], got[chips // 2 - 1 : -1]
    counts = len(early), len(late)
    face, corner = (slots + slots // 4, HALF, LANES), ((slots + 2) * COMP, LANES)
    corners = shape(*face), shape(*corner), shape(*corner)
    up_early, *down = pl.pallas_call(
        lambda *refs: early_kernel(cap, counts[0], *refs),
        out_shape=(shape(bundle_rows(cap, counts[0])[-1], LANES), *corners),
        in_specs=[VMEM] * counts[0],
        out_specs=(VMEM,) * 4,
        name="early",
        compiler_params=params,
    )(*early)
    up_late = shape(bundle_rows(cap, counts[1])[-1], LANES)
    going = pl.pallas_call(
        lambda *refs: next_kernel(cap, *refs),
        out_shape=(up_late, *corners),
        in_specs=[VMEM] * (counts[1] + 2),
        out_specs=(VMEM,) * 4,
        input_output_aliases={counts[1] - 1 + n: 1 + n for n in range(3)},
        name="next",
        compiler_params=params,
    )(*late[:-1], *inside(*down))
    up_late, down, *_ = pl.pallas_call(
        lambda *refs: last_kernel(cap, slots, counts[1], *refs),
        out_shape=(up_late, *corners),
        in_specs=[VMEM] * 5,
        out_specs=(VMEM,) * 4,
        input_output_aliases={1 + n: n for n in range(4)},
        name="last",
        compiler_params=params,
    )(late[-1], *inside(*going))
    forward = [(i, (i + 1) % groups) for i in range(groups)]
    backward = [(j, i) for i, j in forward]
    from_below = [lax.ppermute(up, "grp", forward) for up in (up_early, up_late)]
    above = lax.ppermute(down, "grp", backward)
    below = pl.pallas_call(
        lambda *refs: catch_kernel(cap, slots, counts, *refs),
        out_shape=shape(*face),
        in_specs=[VMEM],
        out_specs=VMEM,
        scratch_shapes=[pltpu.VMEM(corner, f32)] * 2,
        name="catch",
        compiler_params=params,
    )(*inside(jnp.concatenate(from_below)))
    work = pl.pallas_call(
        lambda *refs: inner_kernel(cap, slots, peers, *refs),
        out_shape=shape(ENTRIES, COMP, DEPTH, LANES),
        in_specs=[VMEM] * chips + [SMEM, VMEM],
        out_specs=VMEM,
        scratch_shapes=[pltpu.VMEM((slots + 1, ROWS, LANES), f32)] * 3,
        name="inner",
        compiler_params=params,
    )(*got, table, weights)
    return pl.pallas_call(
        lambda *refs: outer_kernel(slots, *refs),
        out_shape=(jax.ShapeDtypeStruct(fields.shape, f32), shape(*work.shape)),
        in_specs=[VMEM] * 2 + [SMEM] + [VMEM] * 2,
        out_specs=(pl.BlockSpec(memory_space=pl.ANY), VMEM),
        input_output_aliases={4: 1},
        scratch_shapes=[
            pltpu.VMEM((slots, COMP, 2 * LANES), f32),
            pltpu.VMEM((2, slots, COMP, LANES), f32),
            pltpu.SemaphoreType.DMA((3,)),
        ],
        name="outer",
        compiler_params=params,
    )(*inside(below, above), table, weights, *inside(work))[0]


def solution(mesh):
    placed = (P(("grp", "loc"), None, None), P(("grp", "loc")), P(), P(), P())
    return jax.shard_map(
        per_device,
        mesh=mesh,
        in_specs=placed,
        out_specs=P(("grp", "loc"), None, None),
        check_vma=False,
    )
```

```python
import jax
import jax.numpy as jnp
from jax import lax
from jax.experimental import pallas as pl
from jax.experimental.pallas import tpu as pltpu
from jax.sharding import PartitionSpec as P

COMP = 4
LANES = 128
CHUNKS = 4
ROWS = CHUNKS * COMP
HALF = ROWS // 2
TOP = 8
DEPTH = 32
PAIRS = [(i, j) for i in range(COMP) for j in range(i + 1, COMP)]
TABLE = COMP + COMP * COMP + 3 * len(PAIRS)

VMEM = pl.BlockSpec(memory_space=pltpu.VMEM)
SMEM = pl.BlockSpec(memory_space=pltpu.SMEM)


def lane_parts(shape):
    lane = lax.broadcasted_iota(jnp.int32, shape, 1)
    return lane // 64, (lane // 8) % 8, lane % 8


def turn(v, shift):
    return pltpu.roll(v, shift % LANES, 1)


def route(peers, cap, slots, goal_of, held, label, count):
    for peer in range(peers):
        count[peer] = 0
        for k in range(cap):
            held[peer * cap + k] = 0
            label[peer * cap + k] = slots
    for i in range(slots):
        goal = goal_of(i)
        peer = lax.div(goal, slots)
        k = count[peer]
        count[peer] = k + 1
        held[peer * cap + k] = i
        label[peer * cap + k] = lax.rem(goal, slots)


def other_route_kernel(peers, cap, slots, target, held, label, count):
    goals = target[...]
    route(peers, cap, slots, lambda i: goals[0, i], held, label, count)


def pack_kernel(peers, cap, flip, held, label, other_held, other_label, fields, other_fields, out, *weights):
    _, y, _ = lane_parts((COMP, LANES))
    row = lax.broadcasted_iota(jnp.int32, (8, LANES), 1)
    peer = lax.axis_index("loc") ^ flip
    places = [lax.rem(peer + d, peers) * cap for d in (0, 1, peers - 1)]
    names = jnp.zeros((8, LANES), jnp.int32)
    for core, (source, held, label) in enumerate(((fields, held, label), (other_fields, other_held, other_label))):
        for k in range(cap):
            own, high, low = [held[at + k] for at in places]
            entry = core * cap + k
            for n, at in enumerate(places):
                names = jnp.where(row == 2 * cap * n + entry, label[at + k], names)
            for chunk in range(CHUNKS):
                part = slice(chunk * LANES, (chunk + 1) * LANES)
                at = entry * ROWS + chunk * COMP
                out[at : at + COMP, :] = source[own, :, part]
                at += 2 * cap * ROWS
                out[at : at + COMP, :] = jnp.where(y < 4, source[high, :, part], source[low, :, part])
    out[4 * cap * ROWS :, :] = names.astype(jnp.float32)
    if weights:
        fill_weights(weights[0])


def fill_weights(out):
    shape = (LANES, LANES)
    z, y, x = lane_parts(shape)
    source = lax.broadcasted_iota(jnp.int32, shape, 0)
    dz, dy, dx = source // 64 - z, (source // 8) % 8 - y, source % 8 - x

    def stencil(d):
        return jnp.where(jnp.abs(d) == 1, 16.0, jnp.where(jnp.abs(d) == 2, -1.0, 0.0))

    def only(mask, value):
        return jnp.where(mask, value, 0.0)

    swap = only((dz != 0) & (dy == 0) & (dx == 0), 16.0)
    along_y, along_x = (dz == 0) & (dx == 0), (dz == 0) & (dy == 0)
    parts = (
        swap + only(along_y, stencil(dy)) + only(along_x, stencil(dx)),
        only(along_y, stencil(dy + 8) + stencil(dy - 8)),
        only(along_x, stencil(dx + 8) + stencil(dx - 8)),
        swap,
    )
    for n, part in enumerate(parts):
        out[n * LANES : (n + 1) * LANES, :] = part.astype(out.dtype)


def entries(cap, got):
    for message in got:
        names = message[4 * cap * ROWS : 4 * cap * ROWS + 1, :].astype(jnp.int32)
        for k in range(2 * cap):
            yield message, k * ROWS, (2 * cap + k) * ROWS, names[0, k], names[0, 2 * cap + k], names[0, 4 * cap + k]


def squeeze(one, two, y):
    return jnp.where((y >= 2) & (y < 6), jnp.where(y < 4, turn(two, 16), turn(two, -16)), one)


def second_of(both, y):
    return jnp.where(y < 4, turn(both, -16), turn(both, 16))


def bundle_rows(cap, count):
    corners = 2 * cap * count * HALF
    names = corners + cap * count * COMP
    return corners, names, names + 8 * ((count + 7) // 8)


def bundle(cap, count, got, out, before=0):
    corners, names, end = bundle_rows(cap, count)
    _, y, _ = lane_parts((COMP, LANES))
    if before == 0:
        out[names:, :] = jnp.zeros((end - names, LANES), out.dtype)
    for n, message in enumerate(got, before):
        for k in range(2 * cap):
            at = (2 * cap * n + k) * HALF
            out[at : at + HALF, :] = message[k * ROWS + HALF : (k + 1) * ROWS, :]
        for k in range(cap):
            one, two = [message[(2 * cap + e + 1) * ROWS - COMP : (2 * cap + e + 1) * ROWS, :] for e in (k, cap + k)]
            at = corners + (cap * n + k) * COMP
            out[at : at + COMP, :] = squeeze(one, two, y)
        out[names + n : names + n + 1, :] = message[4 * cap * ROWS : 4 * cap * ROWS + 1, :]


def put_down(cap, got, down, high, low):
    for message, whole, joined, slot, high_slot, low_slot in entries(cap, got):
        down[slot] = message[whole : whole + HALF, :]
        put_corner(message[joined : joined + COMP, :], high, high_slot, low, low_slot)


def put_corner(rows, high, high_slot, low, low_slot):
    high[pl.ds(pl.multiple_of(high_slot * COMP, COMP), COMP), :] = rows
    low[pl.ds(pl.multiple_of(low_slot * COMP, COMP), COMP), :] = rows


def put_sides(slots, faces, high, low):
    half = slots // 2 * COMP
    _, y, _ = lane_parts((half, LANES))
    one, two = [jnp.where(y < 4, high[at : at + half, :], low[at : at + half, :]) for at in (0, half)]
    both = squeeze(one, two, y)
    for n in range(half // HALF):
        faces[slots + n] = both[n * HALF : (n + 1) * HALF]


def early_kernel(cap, count, *refs):
    got, (up, down, high, low) = refs[:-4], refs[-4:]
    bundle(cap, count, got, up)
    put_down(cap, got, down, high, low)


def next_kernel(cap, *refs):
    got, (up, down, high, low) = refs[:-7], refs[-4:]
    bundle(cap, len(got) + 1, got, up)
    put_down(cap, got, down, high, low)


def last_kernel(cap, slots, count, message, *refs):
    up, down, high, low = refs[-4:]
    bundle(cap, count, [message], up, count - 1)
    put_down(cap, [message], down, high, low)
    put_sides(slots, down, high, low)


def catch_kernel(cap, slots, counts, *refs):
    joined, faces, high, low = refs
    split = bundle_rows(cap, counts[0])[-1]
    refs = joined.at[:split], joined.at[split:]
    _, y, _ = lane_parts((COMP, LANES))
    for ref, count in zip(refs, counts):
        corners, names, _ = bundle_rows(cap, count)
        for n in range(count):
            slot_of = ref[names + n : names + n + 1, :].astype(jnp.int32)
            for k in range(2 * cap):
                at = (2 * cap * n + k) * HALF
                faces[slot_of[0, k]] = ref[at : at + HALF, :]
                at = corners + (cap * n + k % cap) * COMP
                rows = ref[at : at + COMP, :]
                if k >= cap:
                    rows = second_of(rows, y)
                put_corner(rows, high, slot_of[0, 2 * cap + k], low, slot_of[0, 4 * cap + k])
    put_sides(slots, faces, high, low)


def stage_kernel(peers, cap, slots, *refs):
    arguments, (out, held, label, table), inside, (count, sems) = refs[:5], refs[5:9], refs[9:13], refs[13:]
    copies = [pltpu.make_async_copy(a, b, sems.at[n]) for n, (a, b) in enumerate(zip(arguments, (out, *inside)))]
    for copy in copies[1:] + copies[:1]:
        copy.start()
    for copy in copies[1:]:
        copy.wait()
    target, gradient, relaxation, interaction = inside
    route(peers, cap, slots, lambda i: target[i], held, label, count)
    for i in range(COMP):
        rate = relaxation[i]
        table[i] = rate
        for j in range(COMP):
            table[COMP + i * COMP + j] = rate * gradient[i, j] * (1.0 / 12.0)
    at = COMP + COMP * COMP
    for i, j in PAIRS:
        for order in range(3):
            table[at] = interaction[order, i, j]
            at += 1
    copies[0].wait()


def coefficients(table):
    rates = [table[i] for i in range(COMP)]
    mixing = [[table[COMP + i * COMP + j] for j in range(COMP)] for i in range(COMP)]
    at = COMP + COMP * COMP
    pairs = {pair: [table[at + 3 * n + order] for order in range(3)] for n, pair in enumerate(PAIRS)}
    return rates, mixing, pairs


def mixed(start, laps, mixing):
    result = []
    for i in range(COMP):
        total = start[i]
        for j in range(COMP):
            total += mixing[i][j] * laps[j]
        result.append(total)
    return result


def pieces(values):
    rest = jnp.concatenate(values, axis=0)
    result = []
    for n in range(3):
        piece = rest.astype(jnp.bfloat16)
        result.append(piece)
        rest = rest - piece.astype(jnp.float32)
    return result


def steps(chunks, weights, scalars):
    rates, mixing, pairs = scalars
    layer, _, x = lane_parts(chunks[0][0][0].shape)
    slots = chunks[0][0][0].shape[0]
    rows = []
    for v, ahead, behind, above, below, beside in chunks:
        ends = [jnp.where(x < 4, a, b) for a, b in zip(ahead, behind)]
        layers = [jnp.where(layer == 0, a, b) for a, b in zip(above, below)]
        rows += [jnp.concatenate(p, axis=1) for p in zip(*[pieces(part) for part in (v, beside, ends, layers)])]
    sums = jnp.dot(jnp.concatenate(rows, axis=0), weights[...], preferred_element_type=jnp.float32)
    count = COMP * slots
    results = []
    for n, (v, _, _, above, below, _) in enumerate(chunks):
        near = sum(sums[(3 * n + m) * count : (3 * n + m + 1) * count] for m in range(3))
        laps = [near[c * slots : (c + 1) * slots] - (above[c] + below[c]) - 90.0 * v[c] for c in range(COMP)]
        drive = [None] * COMP
        for (i, j), (a, b, c) in pairs.items():
            gap = v[i] - v[j]
            bend = c * gap
            slope = b + bend
            energy = a + slope * gap
            cross = v[i] * v[j] * (slope + bend)
            first = v[j] * energy + cross
            second = v[i] * energy - cross
            drive[i] = first if drive[i] is None else drive[i] + first
            drive[j] = second if drive[j] is None else drive[j] + second
        results.append(mixed([v[i] - rates[i] * drive[i] for i in range(COMP)], laps, mixing))
    return results


def store(slots, ref, at, values):
    for c, value in enumerate(values):
        ref[at, c, TOP : TOP + slots, :] = value
        ref[at, c, TOP - 1 : TOP, :] = value[slots - 1 :]
        ref[at, c, TOP + slots : TOP + slots + 1, :] = value[:1]


def load(slots, ref, at, offset=0):
    return [ref[at, c, TOP + offset : TOP + offset + slots, :] for c in range(COMP)]


def move(slots, work, places, weights, scalars):
    chunks = []
    for at, above, below, beside, _ in places:
        around = [load(slots, work, n) for n in (above, below, beside)]
        chunks.append((load(slots, work, at), load(slots, work, at, 1), load(slots, work, at, -1), *around))
    for place, values in zip(places, steps(chunks, weights, scalars)):
        store(slots, work, place[-1], values)


def column(ref, start, count, stride):
    flat = ref.reshape(ref.shape[0] * ref.shape[1], LANES)
    return flat[pl.ds(start, count, stride=stride), :]


SPAN = CHUNKS + 2
BLOCK, SIDE, BLOCK_NEXT, SIDE_NEXT, FINAL, BEYOND = [n * SPAN for n in range(5)] + [4 * SPAN + 2]
ENTRIES = BEYOND + 2


def inner_kernel(cap, slots, peers, *refs):
    got, (table, weights, work, block, high, low) = refs[: peers // 2], refs[peers // 2 :]
    scalars = coefficients(table)
    _, y, _ = lane_parts((slots, LANES))
    for message, whole, joined, slot, high_slot, low_slot in entries(cap, got):
        block[slot] = message[whole : whole + ROWS, :]
        rows = message[joined : joined + ROWS, :]
        high[high_slot] = rows
        low[low_slot] = rows
    for base in range(0, FINAL, SPAN):
        for at in (base, base + SPAN - 1):
            work[at] = jnp.zeros(work.shape[1:], work.dtype)

    @pl.loop(0, CHUNKS)
    def _(k):
        rows = [k * COMP + c for c in range(COMP)]
        store(slots, work, BLOCK + 1 + k, [column(block, r, slots, ROWS) for r in rows])
        sides = [jnp.where(y < 4, column(high, r, slots, ROWS), column(low, r, slots, ROWS)) for r in rows]
        store(slots, work, SIDE + 1 + k, sides)

    @pl.loop(0, 2)
    def _(side):
        places = []
        for k in range(1, CHUNKS + 1):
            at = side * SPAN + k
            places.append((at, at + 1, at - 1, (1 - side) * SPAN + k, BLOCK_NEXT + at))
        move(slots, work, places, weights, scalars)

    second, third = BLOCK_NEXT + 2, BLOCK_NEXT + 3
    places = [
        (second, third, BLOCK_NEXT, SIDE_NEXT + 2, FINAL),
        (third, BLOCK_NEXT + SPAN - 1, second, SIDE_NEXT + 3, FINAL + 1),
    ]
    move(slots, work, places, weights, scalars)


def outer_kernel(slots, below, above, table, weights, _, out, work, middle, ends, sems):
    scalars = coefficients(table)
    mixing = scalars[1]
    pairs = slots // 2
    last = SPAN - 1
    _, y, _ = lane_parts((pairs, LANES))
    layer, _, _ = lane_parts((slots, LANES))

    def add(start, beyond, end):
        laps = [16.0 * turn(jnp.where(layer == 1 - end, b, 0.0), 64) - b for b in beyond]
        return mixed(start, laps, mixing)

    for end, ref in enumerate((below, above)):
        near, distant, side = [], [], []
        for c in range(COMP):
            near.append(column(ref, (1 - end) * COMP + c, slots, HALF))
            distant.append(column(ref, end * COMP + c, slots, HALF))
            both = column(ref, slots * HALF + c, pairs, COMP)
            side.append(jnp.concatenate([both, second_of(both, y)], axis=0))
        edge = 1 + end * (CHUNKS - 1)
        store(slots, work, BLOCK + end * last, near)
        store(slots, work, BEYOND + end, distant)
        store(slots, work, SIDE + end * last, side)
        first = add(load(slots, work, BLOCK_NEXT + edge), near, end)
        store(slots, work, SIDE_NEXT + edge, add(load(slots, work, SIDE_NEXT + edge), side, end))
        store(slots, work, BLOCK_NEXT + edge, first)
        for c, value in enumerate(add(load(slots, work, FINAL + end), first, end)):
            middle[:, c, end * LANES : (end + 1) * LANES] = value

    copies = [pltpu.make_async_copy(middle, out.at[:, :, LANES : 3 * LANES], sems.at[2])]
    copies[0].start()

    @pl.loop(0, 2)
    def _(late):
        places = []
        for end in range(2):
            outside = end * last
            at = jnp.where(late == 1, BLOCK_NEXT + 1 + end * (CHUNKS - 1), BLOCK + outside)
            beyond = jnp.where(late == 1, BLOCK_NEXT + outside, BEYOND + end)
            beside = jnp.where(late == 1, SIDE_NEXT + 1 + end * (CHUNKS - 1), SIDE + outside)
            to = jnp.where(late == 1, BLOCK, BLOCK_NEXT) + outside
            up, down = (beyond, at - 1) if end else (at + 1, beyond)
            places.append((at, up, down, beside, to))
        move(slots, work, places, weights, scalars)

    for end in range(2):
        for c, value in enumerate(load(slots, work, BLOCK + end * last)):
            ends[end, :, c, :] = value
        at = end * (CHUNKS - 1) * LANES
        copies.append(pltpu.make_async_copy(ends.at[end], out.at[:, :, at : at + LANES], sems.at[end]))
        copies[-1].start()
    for copy in copies:
        copy.wait()


def per_device(fields, target, gradient_matrix, relaxation, interaction):
    slots = fields.shape[0]
    peers = lax.axis_size("loc")
    groups = lax.axis_size("grp")
    cap = (slots + peers - 1) // peers
    chips = peers // 2
    f32 = jnp.float32
    params = pltpu.CompilerParams(vmem_limit_bytes=8 << 20)

    def shape(*dims):
        return pltpu.VMEM(dims, f32)

    def inside(*arrays):
        return [pltpu.with_memory_space_constraint(a, pltpu.VMEM) for a in arrays]

    def cross(array, flip):
        return lax.ppermute(array, "loc", [(i, i ^ flip) for i in range(peers)])

    numbers = pltpu.SMEM((peers * cap,), jnp.int32)
    arguments = fields, target, gradient_matrix, relaxation, interaction
    staged, held, label, table = pl.pallas_call(
        lambda *refs: stage_kernel(peers, cap, slots, *refs),
        out_shape=(shape(*fields.shape), numbers, numbers, pltpu.SMEM((TABLE,), f32)),
        in_specs=[pl.BlockSpec(memory_space=pl.ANY)] * 5,
        out_specs=(VMEM, SMEM, SMEM, SMEM),
        scratch_shapes=[pltpu.SMEM(a.shape, a.dtype) for a in arguments[1:]]
        + [pltpu.SMEM((peers,), jnp.int32), pltpu.SemaphoreType.DMA((5,))],
        name="stage",
    )(*arguments)
    table = pltpu.with_memory_space_constraint(table, pltpu.SMEM)
    other_fields, other_target = cross(fields, 1), cross(target.reshape(1, slots), 1)
    other = pl.pallas_call(
        lambda *refs: other_route_kernel(peers, cap, slots, *refs),
        out_shape=(numbers, numbers),
        in_specs=[VMEM],
        out_specs=(SMEM,) * 2,
        scratch_shapes=[pltpu.SMEM((peers,), jnp.int32)],
        name="route",
        compiler_params=params,
    )(*inside(other_target))
    routes = [pltpu.with_memory_space_constraint(a, pltpu.SMEM) for a in (held, label, *other)]

    def pack(flip):
        message = shape(4 * cap * ROWS + 8, LANES)
        extra = () if flip else (pltpu.VMEM((4 * LANES, LANES), jnp.bfloat16),)
        return pl.pallas_call(
            lambda *refs: pack_kernel(peers, cap, flip, *refs),
            out_shape=(message, *extra),
            in_specs=[SMEM] * 4 + [VMEM] * 2,
            out_specs=(VMEM,) * (1 + len(extra)),
            name="pack",
            compiler_params=params,
        )(*routes, *inside(staged, other_fields))

    flips = [2 * j + 1 for j in reversed(range(1, chips))] + [0]
    *sent, (own, weights) = [pack(flip) for flip in flips]
    weights = inside(weights)[0]
    got = inside(*[cross(message, flip) for (message,), flip in zip(sent, flips)], own)
    early, late = got[: chips // 2 - 1] + got[-1:], got[chips // 2 - 1 : -1]
    counts = len(early), len(late)
    face, corner = (slots + slots // 4, HALF, LANES), ((slots + 2) * COMP, LANES)
    corners = shape(*face), shape(*corner), shape(*corner)
    up_early, *down = pl.pallas_call(
        lambda *refs: early_kernel(cap, counts[0], *refs),
        out_shape=(shape(bundle_rows(cap, counts[0])[-1], LANES), *corners),
        in_specs=[VMEM] * counts[0],
        out_specs=(VMEM,) * 4,
        name="early",
        compiler_params=params,
    )(*early)
    up_late = shape(bundle_rows(cap, counts[1])[-1], LANES)
    going = pl.pallas_call(
        lambda *refs: next_kernel(cap, *refs),
        out_shape=(up_late, *corners),
        in_specs=[VMEM] * (counts[1] + 2),
        out_specs=(VMEM,) * 4,
        input_output_aliases={counts[1] - 1 + n: 1 + n for n in range(3)},
        name="next",
        compiler_params=params,
    )(*late[:-1], *inside(*down))
    up_late, down, *_ = pl.pallas_call(
        lambda *refs: last_kernel(cap, slots, counts[1], *refs),
        out_shape=(up_late, *corners),
        in_specs=[VMEM] * 5,
        out_specs=(VMEM,) * 4,
        input_output_aliases={1 + n: n for n in range(4)},
        name="last",
        compiler_params=params,
    )(late[-1], *inside(*going))
    forward = [(i, (i + 1) % groups) for i in range(groups)]
    backward = [(j, i) for i, j in forward]
    from_below = [lax.ppermute(up, "grp", forward) for up in (up_early, up_late)]
    above = lax.ppermute(down, "grp", backward)
    below = pl.pallas_call(
        lambda *refs: catch_kernel(cap, slots, counts, *refs),
        out_shape=shape(*face),
        in_specs=[VMEM],
        out_specs=VMEM,
        scratch_shapes=[pltpu.VMEM(corner, f32)] * 2,
        name="catch",
        compiler_params=params,
    )(*inside(jnp.concatenate(from_below)))
    work = pl.pallas_call(
        lambda *refs: inner_kernel(cap, slots, peers, *refs),
        out_shape=shape(ENTRIES, COMP, DEPTH, LANES),
        in_specs=[VMEM] * chips + [SMEM, VMEM],
        out_specs=VMEM,
        scratch_shapes=[pltpu.VMEM((slots + 1, ROWS, LANES), f32)] * 3,
        name="inner",
        compiler_params=params,
    )(*got, table, weights)
    return pl.pallas_call(
        lambda *refs: outer_kernel(slots, *refs),
        out_shape=(jax.ShapeDtypeStruct(fields.shape, f32), shape(*work.shape)),
        in_specs=[VMEM] * 2 + [SMEM] + [VMEM] * 2,
        out_specs=(pl.BlockSpec(memory_space=pl.ANY), VMEM),
        input_output_aliases={4: 1},
        scratch_shapes=[
            pltpu.VMEM((slots, COMP, 2 * LANES), f32),
            pltpu.VMEM((2, slots, COMP, LANES), f32),
            pltpu.SemaphoreType.DMA((3,)),
        ],
        name="outer",
        compiler_params=params,
    )(*inside(below, above), table, weights, *inside(work))[0]


def solution(mesh):
    placed = (P(("grp", "loc"), None, None), P(("grp", "loc")), P(), P(), P())
    return jax.shard_map(
        per_device,
        mesh=mesh,
        in_specs=placed,
        out_specs=P(("grp", "loc"), None, None),
        check_vma=False,
    )
```

```python
import jax
import jax.numpy as jnp
from jax import lax
from jax.experimental import pallas as pl
from jax.experimental.pallas import tpu as pltpu
from jax.sharding import PartitionSpec as P

COMP = 4
LANES = 128
CHUNKS = 4
ROWS = CHUNKS * COMP
HALF = ROWS // 2
TOP = 8
DEPTH = 32
PAIRS = [(i, j) for i in range(COMP) for j in range(i + 1, COMP)]
TABLE = COMP + COMP * COMP + 3 * len(PAIRS)

VMEM = pl.BlockSpec(memory_space=pltpu.VMEM)
SMEM = pl.BlockSpec(memory_space=pltpu.SMEM)


def lane_parts(shape):
    lane = lax.broadcasted_iota(jnp.int32, shape, 1)
    return lane // 64, (lane // 8) % 8, lane % 8


def turn(v, shift):
    return pltpu.roll(v, shift % LANES, 1)


def route(peers, cap, slots, goal_of, held, label, count):
    for peer in range(peers):
        count[peer] = peer * cap
        if peers * cap > slots:
            for k in range(cap):
                held[peer * cap + k] = 0
                label[peer * cap + k] = slots
    for i in range(slots):
        peer, slot = goal_of(i)
        at = count[peer]
        count[peer] = at + 1
        held[at] = i
        label[at] = slot


def other_route_kernel(peers, cap, slots, target, held, label, count):
    goals = target[...]
    homes, places = lax.div(goals, slots), lax.rem(goals, slots)
    route(peers, cap, slots, lambda i: (homes[0, i], places[0, i]), held, label, count)


def pack_kernel(peers, cap, flip, held, label, other_held, other_label, fields, other_fields, out, *weights):
    _, y, _ = lane_parts((COMP, LANES))
    row = lax.broadcasted_iota(jnp.int32, (8, LANES), 1)
    peer = lax.axis_index("loc") ^ flip
    places = [lax.rem(peer + d, peers) * cap for d in (0, 1, peers - 1)]
    names = jnp.zeros((8, LANES), jnp.int32)
    for core, (source, held, label) in enumerate(((fields, held, label), (other_fields, other_held, other_label))):
        for k in range(cap):
            own, high, low = [held[at + k] for at in places]
            entry = core * cap + k
            for n, at in enumerate(places):
                names = jnp.where(row == 2 * cap * n + entry, label[at + k], names)
            for chunk in range(CHUNKS):
                part = slice(chunk * LANES, (chunk + 1) * LANES)
                at = entry * ROWS + chunk * COMP
                out[at : at + COMP, :] = source[own, :, part]
                at += 2 * cap * ROWS
                out[at : at + COMP, :] = jnp.where(y < 4, source[high, :, part], source[low, :, part])
    out[4 * cap * ROWS :, :] = names.astype(jnp.float32)
    if weights:
        fill_weights(weights[0])


def fill_weights(out):
    shape = (LANES, LANES)
    z, y, x = lane_parts(shape)
    source = lax.broadcasted_iota(jnp.int32, shape, 0)
    dz, dy, dx = source // 64 - z, (source // 8) % 8 - y, source % 8 - x

    def stencil(d):
        return jnp.where(jnp.abs(d) == 1, 16.0, jnp.where(jnp.abs(d) == 2, -1.0, 0.0))

    def only(mask, value):
        return jnp.where(mask, value, 0.0)

    swap = only((dz != 0) & (dy == 0) & (dx == 0), 16.0)
    along_y, along_x = (dz == 0) & (dx == 0), (dz == 0) & (dy == 0)
    parts = (
        swap + only(along_y, stencil(dy)) + only(along_x, stencil(dx)),
        only(along_y, stencil(dy + 8) + stencil(dy - 8)),
        only(along_x, stencil(dx + 8) + stencil(dx - 8)),
        swap,
    )
    for n, part in enumerate(parts):
        out[n * LANES : (n + 1) * LANES, :] = part.astype(out.dtype)


def entries(cap, got):
    for message in got:
        names = message[4 * cap * ROWS : 4 * cap * ROWS + 1, :].astype(jnp.int32)
        for k in range(2 * cap):
            yield message, k * ROWS, (2 * cap + k) * ROWS, names[0, k], names[0, 2 * cap + k], names[0, 4 * cap + k]


def squeeze(one, two, y):
    return jnp.where((y >= 2) & (y < 6), jnp.where(y < 4, turn(two, 16), turn(two, -16)), one)


def second_of(both, y):
    return jnp.where(y < 4, turn(both, -16), turn(both, 16))


def bundle_rows(cap, count):
    corners = 2 * cap * count * HALF
    names = corners + cap * count * COMP
    return corners, names, names + 8 * ((count + 7) // 8)


def bundle(cap, count, got, out, before=0):
    corners, names, end = bundle_rows(cap, count)
    _, y, _ = lane_parts((COMP, LANES))
    if before == 0:
        out[names:, :] = jnp.zeros((end - names, LANES), out.dtype)
    for n, message in enumerate(got, before):
        for k in range(2 * cap):
            at = (2 * cap * n + k) * HALF
            out[at : at + HALF, :] = message[k * ROWS + HALF : (k + 1) * ROWS, :]
        for k in range(cap):
            one, two = [message[(2 * cap + e + 1) * ROWS - COMP : (2 * cap + e + 1) * ROWS, :] for e in (k, cap + k)]
            at = corners + (cap * n + k) * COMP
            out[at : at + COMP, :] = squeeze(one, two, y)
        out[names + n : names + n + 1, :] = message[4 * cap * ROWS : 4 * cap * ROWS + 1, :]


def put_down(cap, got, down, high, low):
    for message, whole, joined, slot, high_slot, low_slot in entries(cap, got):
        down[slot] = message[whole : whole + HALF, :]
        put_corner(message[joined : joined + COMP, :], high, high_slot, low, low_slot)


def put_corner(rows, high, high_slot, low, low_slot):
    high[pl.ds(pl.multiple_of(high_slot * COMP, COMP), COMP), :] = rows
    low[pl.ds(pl.multiple_of(low_slot * COMP, COMP), COMP), :] = rows


def put_sides(slots, faces, high, low):
    half = slots // 2 * COMP
    _, y, _ = lane_parts((half, LANES))
    one, two = [jnp.where(y < 4, high[at : at + half, :], low[at : at + half, :]) for at in (0, half)]
    both = squeeze(one, two, y)
    for n in range(half // HALF):
        faces[slots + n] = both[n * HALF : (n + 1) * HALF]


def early_kernel(cap, count, *refs):
    got, (up, down, high, low) = refs[:-4], refs[-4:]
    bundle(cap, count, got, up)
    put_down(cap, got, down, high, low)


def next_kernel(cap, *refs):
    got, (up, down, high, low) = refs[:-7], refs[-4:]
    bundle(cap, len(got) + 1, got, up)
    put_down(cap, got, down, high, low)


def last_kernel(cap, slots, count, message, *refs):
    up, down, high, low = refs[-4:]
    bundle(cap, count, [message], up, count - 1)
    put_down(cap, [message], down, high, low)
    put_sides(slots, down, high, low)


def catch_kernel(cap, slots, counts, *refs):
    joined, faces, high, low = refs
    split = bundle_rows(cap, counts[0])[-1]
    refs = joined.at[:split], joined.at[split:]
    _, y, _ = lane_parts((COMP, LANES))
    for ref, count in zip(refs, counts):
        corners, names, _ = bundle_rows(cap, count)
        for n in range(count):
            slot_of = ref[names + n : names + n + 1, :].astype(jnp.int32)
            for k in range(2 * cap):
                at = (2 * cap * n + k) * HALF
                faces[slot_of[0, k]] = ref[at : at + HALF, :]
                at = corners + (cap * n + k % cap) * COMP
                rows = ref[at : at + COMP, :]
                if k >= cap:
                    rows = second_of(rows, y)
                put_corner(rows, high, slot_of[0, 2 * cap + k], low, slot_of[0, 4 * cap + k])
    put_sides(slots, faces, high, low)


def stage_kernel(peers, cap, slots, *refs):
    arguments, (out, held, label, table), inside, (count, sems) = refs[:5], refs[5:9], refs[9:13], refs[13:]
    copies = [pltpu.make_async_copy(a, b, sems.at[n]) for n, (a, b) in enumerate(zip(arguments, (out, *inside)))]
    for copy in copies[1:] + copies[:1]:
        copy.start()
    for copy in copies[1:]:
        copy.wait()
    target, gradient, relaxation, interaction = inside
    route(peers, cap, slots, lambda i: (lax.div(target[i], slots), lax.rem(target[i], slots)), held, label, count)
    for i in range(COMP):
        rate = relaxation[i]
        table[i] = rate
        for j in range(COMP):
            table[COMP + i * COMP + j] = rate * gradient[i, j] * (1.0 / 12.0)
    at = COMP + COMP * COMP
    for i, j in PAIRS:
        for order in range(3):
            table[at] = interaction[order, i, j]
            at += 1
    copies[0].wait()


def coefficients(table):
    rates = [table[i] for i in range(COMP)]
    mixing = [[table[COMP + i * COMP + j] for j in range(COMP)] for i in range(COMP)]
    at = COMP + COMP * COMP
    pairs = {pair: [table[at + 3 * n + order] for order in range(3)] for n, pair in enumerate(PAIRS)}
    return rates, mixing, pairs


def mixed(start, laps, mixing):
    result = []
    for i in range(COMP):
        total = start[i]
        for j in range(COMP):
            total += mixing[i][j] * laps[j]
        result.append(total)
    return result


def pieces(values):
    rest = jnp.concatenate(values, axis=0)
    result = []
    for n in range(3):
        piece = rest.astype(jnp.bfloat16)
        result.append(piece)
        rest = rest - piece.astype(jnp.float32)
    return result


def steps(chunks, weights, scalars):
    rates, mixing, pairs = scalars
    layer, _, x = lane_parts(chunks[0][0][0].shape)
    slots = chunks[0][0][0].shape[0]
    rows = []
    for v, ahead, behind, above, below, beside in chunks:
        ends = [jnp.where(x < 4, a, b) for a, b in zip(ahead, behind)]
        layers = [jnp.where(layer == 0, a, b) for a, b in zip(above, below)]
        rows += [jnp.concatenate(p, axis=1) for p in zip(*[pieces(part) for part in (v, beside, ends, layers)])]
    sums = jnp.dot(jnp.concatenate(rows, axis=0), weights[...], preferred_element_type=jnp.float32)
    count = COMP * slots
    results = []
    for n, (v, _, _, above, below, _) in enumerate(chunks):
        near = sum(sums[(3 * n + m) * count : (3 * n + m + 1) * count] for m in range(3))
        laps = [near[c * slots : (c + 1) * slots] - (above[c] + below[c]) - 90.0 * v[c] for c in range(COMP)]
        drive = [None] * COMP
        for (i, j), (a, b, c) in pairs.items():
            gap = v[i] - v[j]
            bend = c * gap
            slope = b + bend
            energy = a + slope * gap
            cross = v[i] * v[j] * (slope + bend)
            first = v[j] * energy + cross
            second = v[i] * energy - cross
            drive[i] = first if drive[i] is None else drive[i] + first
            drive[j] = second if drive[j] is None else drive[j] + second
        results.append(mixed([v[i] - rates[i] * drive[i] for i in range(COMP)], laps, mixing))
    return results


def store(slots, ref, at, values):
    for c, value in enumerate(values):
        ref[at, c, TOP : TOP + slots, :] = value
        ref[at, c, TOP - 1 : TOP, :] = value[slots - 1 :]
        ref[at, c, TOP + slots : TOP + slots + 1, :] = value[:1]


def load(slots, ref, at, offset=0):
    return [ref[at, c, TOP + offset : TOP + offset + slots, :] for c in range(COMP)]


def move(slots, work, places, weights, scalars):
    chunks = []
    for at, above, below, beside, _ in places:
        around = [load(slots, work, n) for n in (above, below, beside)]
        chunks.append((load(slots, work, at), load(slots, work, at, 1), load(slots, work, at, -1), *around))
    for place, values in zip(places, steps(chunks, weights, scalars)):
        store(slots, work, place[-1], values)


def column(ref, start, count, stride):
    flat = ref.reshape(ref.shape[0] * ref.shape[1], LANES)
    return flat[pl.ds(start, count, stride=stride), :]


SPAN = CHUNKS + 2
BLOCK, SIDE, BLOCK_NEXT, SIDE_NEXT, FINAL, BEYOND = [n * SPAN for n in range(5)] + [4 * SPAN + 2]
ENTRIES = BEYOND + 2


def inner_kernel(cap, slots, peers, *refs):
    got, (table, weights, work, block, high, low) = refs[: peers // 2], refs[peers // 2 :]
    scalars = coefficients(table)
    _, y, _ = lane_parts((slots, LANES))
    for message, whole, joined, slot, high_slot, low_slot in entries(cap, got):
        block[slot] = message[whole : whole + ROWS, :]
        rows = message[joined : joined + ROWS, :]
        high[high_slot] = rows
        low[low_slot] = rows
    for base in range(0, FINAL, SPAN):
        for at in (base, base + SPAN - 1):
            work[at] = jnp.zeros(work.shape[1:], work.dtype)

    @pl.loop(0, CHUNKS)
    def _(k):
        rows = [k * COMP + c for c in range(COMP)]
        store(slots, work, BLOCK + 1 + k, [column(block, r, slots, ROWS) for r in rows])
        sides = [jnp.where(y < 4, column(high, r, slots, ROWS), column(low, r, slots, ROWS)) for r in rows]
        store(slots, work, SIDE + 1 + k, sides)

    @pl.loop(0, 2)
    def _(side):
        places = []
        for k in range(1, CHUNKS + 1):
            at = side * SPAN + k
            places.append((at, at + 1, at - 1, (1 - side) * SPAN + k, BLOCK_NEXT + at))
        move(slots, work, places, weights, scalars)

    second, third = BLOCK_NEXT + 2, BLOCK_NEXT + 3
    places = [
        (second, third, BLOCK_NEXT, SIDE_NEXT + 2, FINAL),
        (third, BLOCK_NEXT + SPAN - 1, second, SIDE_NEXT + 3, FINAL + 1),
    ]
    move(slots, work, places, weights, scalars)


def outer_kernel(slots, below, above, table, weights, _, out, work, middle, ends, sems):
    scalars = coefficients(table)
    mixing = scalars[1]
    pairs = slots // 2
    last = SPAN - 1
    _, y, _ = lane_parts((pairs, LANES))
    layer, _, _ = lane_parts((slots, LANES))

    def add(start, beyond, end):
        laps = [16.0 * turn(jnp.where(layer == 1 - end, b, 0.0), 64) - b for b in beyond]
        return mixed(start, laps, mixing)

    for end, ref in enumerate((below, above)):
        near, distant, side = [], [], []
        for c in range(COMP):
            near.append(column(ref, (1 - end) * COMP + c, slots, HALF))
            distant.append(column(ref, end * COMP + c, slots, HALF))
            both = column(ref, slots * HALF + c, pairs, COMP)
            side.append(jnp.concatenate([both, second_of(both, y)], axis=0))
        edge = 1 + end * (CHUNKS - 1)
        store(slots, work, BLOCK + end * last, near)
        store(slots, work, BEYOND + end, distant)
        store(slots, work, SIDE + end * last, side)
        first = add(load(slots, work, BLOCK_NEXT + edge), near, end)
        store(slots, work, SIDE_NEXT + edge, add(load(slots, work, SIDE_NEXT + edge), side, end))
        store(slots, work, BLOCK_NEXT + edge, first)
        for c, value in enumerate(add(load(slots, work, FINAL + end), first, end)):
            middle[:, c, end * LANES : (end + 1) * LANES] = value

    copies = [pltpu.make_async_copy(middle, out.at[:, :, LANES : 3 * LANES], sems.at[2])]
    copies[0].start()

    @pl.loop(0, 2)
    def _(late):
        places = []
        for end in range(2):
            outside = end * last
            at = jnp.where(late == 1, BLOCK_NEXT + 1 + end * (CHUNKS - 1), BLOCK + outside)
            beyond = jnp.where(late == 1, BLOCK_NEXT + outside, BEYOND + end)
            beside = jnp.where(late == 1, SIDE_NEXT + 1 + end * (CHUNKS - 1), SIDE + outside)
            to = jnp.where(late == 1, BLOCK, BLOCK_NEXT) + outside
            up, down = (beyond, at - 1) if end else (at + 1, beyond)
            places.append((at, up, down, beside, to))
        move(slots, work, places, weights, scalars)

    for end in range(2):
        for c, value in enumerate(load(slots, work, BLOCK + end * last)):
            ends[end, :, c, :] = value
        at = end * (CHUNKS - 1) * LANES
        copies.append(pltpu.make_async_copy(ends.at[end], out.at[:, :, at : at + LANES], sems.at[end]))
        copies[-1].start()
    for copy in copies:
        copy.wait()


def per_device(fields, target, gradient_matrix, relaxation, interaction):
    slots = fields.shape[0]
    peers = lax.axis_size("loc")
    groups = lax.axis_size("grp")
    cap = (slots + peers - 1) // peers
    chips = peers // 2
    f32 = jnp.float32
    params = pltpu.CompilerParams(vmem_limit_bytes=8 << 20)

    def shape(*dims):
        return pltpu.VMEM(dims, f32)

    def inside(*arrays):
        return [pltpu.with_memory_space_constraint(a, pltpu.VMEM) for a in arrays]

    def cross(array, flip):
        return lax.ppermute(array, "loc", [(i, i ^ flip) for i in range(peers)])

    numbers = pltpu.SMEM((peers * cap,), jnp.int32)
    arguments = fields, target, gradient_matrix, relaxation, interaction
    staged, held, label, table = pl.pallas_call(
        lambda *refs: stage_kernel(peers, cap, slots, *refs),
        out_shape=(shape(*fields.shape), numbers, numbers, pltpu.SMEM((TABLE,), f32)),
        in_specs=[pl.BlockSpec(memory_space=pl.ANY)] * 5,
        out_specs=(VMEM, SMEM, SMEM, SMEM),
        scratch_shapes=[pltpu.SMEM(a.shape, a.dtype) for a in arguments[1:]]
        + [pltpu.SMEM((peers,), jnp.int32), pltpu.SemaphoreType.DMA((5,))],
        name="stage",
    )(*arguments)
    table = pltpu.with_memory_space_constraint(table, pltpu.SMEM)
    other_fields, other_target = cross(fields, 1), cross(target.reshape(1, slots), 1)
    other = pl.pallas_call(
        lambda *refs: other_route_kernel(peers, cap, slots, *refs),
        out_shape=(numbers, numbers),
        in_specs=[VMEM],
        out_specs=(SMEM,) * 2,
        scratch_shapes=[pltpu.SMEM((peers,), jnp.int32)],
        name="route",
        compiler_params=params,
    )(*inside(other_target))
    routes = [pltpu.with_memory_space_constraint(a, pltpu.SMEM) for a in (held, label, *other)]

    def pack(flip):
        message = shape(4 * cap * ROWS + 8, LANES)
        extra = () if flip else (pltpu.VMEM((4 * LANES, LANES), jnp.bfloat16),)
        return pl.pallas_call(
            lambda *refs: pack_kernel(peers, cap, flip, *refs),
            out_shape=(message, *extra),
            in_specs=[SMEM] * 4 + [VMEM] * 2,
            out_specs=(VMEM,) * (1 + len(extra)),
            name="pack",
            compiler_params=params,
        )(*routes, *inside(staged, other_fields))

    flips = [2 * j + 1 for j in reversed(range(1, chips))] + [0]
    *sent, (own, weights) = [pack(flip) for flip in flips]
    weights = inside(weights)[0]
    got = inside(*[cross(message, flip) for (message,), flip in zip(sent, flips)], own)
    early, late = got[: chips // 2 - 1] + got[-1:], got[chips // 2 - 1 : -1]
    counts = len(early), len(late)
    face, corner = (slots + slots // 4, HALF, LANES), ((slots + 2) * COMP, LANES)
    corners = shape(*face), shape(*corner), shape(*corner)
    up_early, *down = pl.pallas_call(
        lambda *refs: early_kernel(cap, counts[0], *refs),
        out_shape=(shape(bundle_rows(cap, counts[0])[-1], LANES), *corners),
        in_specs=[VMEM] * counts[0],
        out_specs=(VMEM,) * 4,
        name="early",
        compiler_params=params,
    )(*early)
    up_late = shape(bundle_rows(cap, counts[1])[-1], LANES)
    going = pl.pallas_call(
        lambda *refs: next_kernel(cap, *refs),
        out_shape=(up_late, *corners),
        in_specs=[VMEM] * (counts[1] + 2),
        out_specs=(VMEM,) * 4,
        input_output_aliases={counts[1] - 1 + n: 1 + n for n in range(3)},
        name="next",
        compiler_params=params,
    )(*late[:-1], *inside(*down))
    up_late, down, *_ = pl.pallas_call(
        lambda *refs: last_kernel(cap, slots, counts[1], *refs),
        out_shape=(up_late, *corners),
        in_specs=[VMEM] * 5,
        out_specs=(VMEM,) * 4,
        input_output_aliases={1 + n: n for n in range(4)},
        name="last",
        compiler_params=params,
    )(late[-1], *inside(*going))
    forward = [(i, (i + 1) % groups) for i in range(groups)]
    backward = [(j, i) for i, j in forward]
    from_below = [lax.ppermute(up, "grp", forward) for up in (up_early, up_late)]
    above = lax.ppermute(down, "grp", backward)
    below = pl.pallas_call(
        lambda *refs: catch_kernel(cap, slots, counts, *refs),
        out_shape=shape(*face),
        in_specs=[VMEM],
        out_specs=VMEM,
        scratch_shapes=[pltpu.VMEM(corner, f32)] * 2,
        name="catch",
        compiler_params=params,
    )(*inside(jnp.concatenate(from_below)))
    work = pl.pallas_call(
        lambda *refs: inner_kernel(cap, slots, peers, *refs),
        out_shape=shape(ENTRIES, COMP, DEPTH, LANES),
        in_specs=[VMEM] * chips + [SMEM, VMEM],
        out_specs=VMEM,
        scratch_shapes=[pltpu.VMEM((slots + 1, ROWS, LANES), f32)] * 3,
        name="inner",
        compiler_params=params,
    )(*got, table, weights)
    return pl.pallas_call(
        lambda *refs: outer_kernel(slots, *refs),
        out_shape=(jax.ShapeDtypeStruct(fields.shape, f32), shape(*work.shape)),
        in_specs=[VMEM] * 2 + [SMEM] + [VMEM] * 2,
        out_specs=(pl.BlockSpec(memory_space=pl.ANY), VMEM),
        input_output_aliases={4: 1},
        scratch_shapes=[
            pltpu.VMEM((slots, COMP, 2 * LANES), f32),
            pltpu.VMEM((2, slots, COMP, LANES), f32),
            pltpu.SemaphoreType.DMA((3,)),
        ],
        name="outer",
        compiler_params=params,
    )(*inside(below, above), table, weights, *inside(work))[0]


def solution(mesh):
    placed = (P(("grp", "loc"), None, None), P(("grp", "loc")), P(), P(), P())
    return jax.shard_map(
        per_device,
        mesh=mesh,
        in_specs=placed,
        out_specs=P(("grp", "loc"), None, None),
        check_vma=False,
    )
```

```python
import jax
import jax.numpy as jnp
from jax import lax
from jax.experimental import pallas as pl
from jax.experimental.pallas import tpu as pltpu
from jax.sharding import PartitionSpec as P

COMP = 4
LANES = 128
CHUNKS = 4
ROWS = CHUNKS * COMP
HALF = ROWS // 2
TOP = 8
DEPTH = 32
PAIRS = [(i, j) for i in range(COMP) for j in range(i + 1, COMP)]
TABLE = COMP + COMP * COMP + 3 * len(PAIRS)

VMEM = pl.BlockSpec(memory_space=pltpu.VMEM)
SMEM = pl.BlockSpec(memory_space=pltpu.SMEM)


def lane_parts(shape):
    lane = lax.broadcasted_iota(jnp.int32, shape, 1)
    return lane // 64, (lane // 8) % 8, lane % 8


def turn(v, shift):
    return pltpu.roll(v, shift % LANES, 1)


def route(peers, cap, slots, goal_of, held, label, count):
    for peer in range(peers):
        count[peer] = peer * cap
        if peers * cap > slots:
            for k in range(cap):
                held[peer * cap + k] = 0
                label[peer * cap + k] = slots
    for i in range(slots):
        peer, slot = goal_of(i)
        at = count[peer]
        count[peer] = at + 1
        held[at] = i
        label[at] = slot


def other_route_kernel(peers, cap, slots, target, held, label, count):
    goals = target[...]
    homes, places = lax.div(goals, slots), lax.rem(goals, slots)
    route(peers, cap, slots, lambda i: (homes[0, i], places[0, i]), held, label, count)


def pack_kernel(peers, cap, flip, held, label, other_held, other_label, fields, other_fields, out, *weights):
    _, y, _ = lane_parts((COMP, LANES))
    row = lax.broadcasted_iota(jnp.int32, (8, LANES), 1)
    peer = lax.axis_index("loc") ^ flip
    places = [lax.rem(peer + d, peers) * cap for d in (0, 1, peers - 1)]
    names = jnp.zeros((8, LANES), jnp.int32)
    for core, (source, held, label) in enumerate(((fields, held, label), (other_fields, other_held, other_label))):
        for k in range(cap):
            own, high, low = [held[at + k] for at in places]
            entry = core * cap + k
            for n, at in enumerate(places):
                names = jnp.where(row == 2 * cap * n + entry, label[at + k], names)
            for chunk in range(CHUNKS):
                part = slice(chunk * LANES, (chunk + 1) * LANES)
                at = entry * ROWS + chunk * COMP
                out[at : at + COMP, :] = source[own, :, part]
                at += 2 * cap * ROWS
                out[at : at + COMP, :] = jnp.where(y < 4, source[high, :, part], source[low, :, part])
    out[4 * cap * ROWS :, :] = names.astype(jnp.float32)
    if weights:
        fill_weights(weights[0])


def fill_weights(out):
    shape = (LANES, LANES)
    z, y, x = lane_parts(shape)
    source = lax.broadcasted_iota(jnp.int32, shape, 0)
    dz, dy, dx = source // 64 - z, (source // 8) % 8 - y, source % 8 - x

    def stencil(d):
        return jnp.where(jnp.abs(d) == 1, 16.0, jnp.where(jnp.abs(d) == 2, -1.0, 0.0))

    def only(mask, value):
        return jnp.where(mask, value, 0.0)

    swap = only((dz != 0) & (dy == 0) & (dx == 0), 16.0)
    along_y, along_x = (dz == 0) & (dx == 0), (dz == 0) & (dy == 0)
    parts = (
        swap + only(along_y, stencil(dy)) + only(along_x, stencil(dx)),
        only(along_y, stencil(dy + 8) + stencil(dy - 8)),
        only(along_x, stencil(dx + 8) + stencil(dx - 8)),
        swap,
    )
    for n, part in enumerate(parts):
        out[n * LANES : (n + 1) * LANES, :] = part.astype(out.dtype)


def entries(cap, got):
    for message in got:
        names = message[4 * cap * ROWS : 4 * cap * ROWS + 1, :].astype(jnp.int32)
        for k in range(2 * cap):
            yield message, k * ROWS, (2 * cap + k) * ROWS, names[0, k], names[0, 2 * cap + k], names[0, 4 * cap + k]


def squeeze(one, two, y):
    return jnp.where((y >= 2) & (y < 6), jnp.where(y < 4, turn(two, 16), turn(two, -16)), one)


def second_of(both, y):
    return jnp.where(y < 4, turn(both, -16), turn(both, 16))


def bundle_rows(cap, count):
    corners = 2 * cap * count * HALF
    names = corners + cap * count * COMP
    return corners, names, names + 8 * ((count + 7) // 8)


def bundle(cap, count, got, out, before=0):
    corners, names, end = bundle_rows(cap, count)
    _, y, _ = lane_parts((COMP, LANES))
    if before == 0:
        out[names:, :] = jnp.zeros((end - names, LANES), out.dtype)
    for n, message in enumerate(got, before):
        for k in range(2 * cap):
            at = (2 * cap * n + k) * HALF
            out[at : at + HALF, :] = message[k * ROWS + HALF : (k + 1) * ROWS, :]
        for k in range(cap):
            one, two = [message[(2 * cap + e + 1) * ROWS - COMP : (2 * cap + e + 1) * ROWS, :] for e in (k, cap + k)]
            at = corners + (cap * n + k) * COMP
            out[at : at + COMP, :] = squeeze(one, two, y)
        out[names + n : names + n + 1, :] = message[4 * cap * ROWS : 4 * cap * ROWS + 1, :]


def put_down(cap, got, down, high, low):
    for message, whole, joined, slot, high_slot, low_slot in entries(cap, got):
        down[slot] = message[whole : whole + HALF, :]
        put_corner(message[joined : joined + COMP, :], high, high_slot, low, low_slot)


def put_corner(rows, high, high_slot, low, low_slot):
    high[pl.ds(pl.multiple_of(high_slot * COMP, COMP), COMP), :] = rows
    low[pl.ds(pl.multiple_of(low_slot * COMP, COMP), COMP), :] = rows


def put_sides(slots, faces, high, low):
    half = slots // 2 * COMP
    _, y, _ = lane_parts((half, LANES))
    one, two = [jnp.where(y < 4, high[at : at + half, :], low[at : at + half, :]) for at in (0, half)]
    both = squeeze(one, two, y)
    for n in range(half // HALF):
        faces[slots + n] = both[n * HALF : (n + 1) * HALF]


def early_kernel(cap, count, *refs):
    got, (up, down, high, low) = refs[:-4], refs[-4:]
    bundle(cap, count, got, up)
    put_down(cap, got, down, high, low)


def next_kernel(cap, *refs):
    got, (up, down, high, low) = refs[:-7], refs[-4:]
    bundle(cap, len(got) + 1, got, up)
    put_down(cap, got, down, high, low)


def last_kernel(cap, slots, count, message, *refs):
    up, down, high, low = refs[-4:]
    bundle(cap, count, [message], up, count - 1)
    put_down(cap, [message], down, high, low)
    put_sides(slots, down, high, low)


def catch_kernel(cap, slots, counts, *refs):
    joined, faces, high, low = refs
    split = bundle_rows(cap, counts[0])[-1]
    refs = joined.at[:split], joined.at[split:]
    _, y, _ = lane_parts((COMP, LANES))
    for ref, count in zip(refs, counts):
        corners, names, _ = bundle_rows(cap, count)
        for n in range(count):
            slot_of = ref[names + n : names + n + 1, :].astype(jnp.int32)
            for k in range(2 * cap):
                at = (2 * cap * n + k) * HALF
                faces[slot_of[0, k]] = ref[at : at + HALF, :]
                at = corners + (cap * n + k % cap) * COMP
                rows = ref[at : at + COMP, :]
                if k >= cap:
                    rows = second_of(rows, y)
                put_corner(rows, high, slot_of[0, 2 * cap + k], low, slot_of[0, 4 * cap + k])
    put_sides(slots, faces, high, low)


def stage_kernel(peers, cap, slots, *refs):
    arguments, (out, held, label, table), inside, (count, sems) = refs[:5], refs[5:9], refs[9:13], refs[13:]
    copies = [pltpu.make_async_copy(a, b, sems.at[n]) for n, (a, b) in enumerate(zip(arguments, (out, *inside)))]
    for copy in copies[1:] + copies[:1]:
        copy.start()
    for copy in copies[1:]:
        copy.wait()
    target, gradient, relaxation, interaction = inside
    route(peers, cap, slots, lambda i: (lax.div(target[i], slots), lax.rem(target[i], slots)), held, label, count)
    for i in range(COMP):
        rate = relaxation[i]
        table[i] = rate
        for j in range(COMP):
            table[COMP + i * COMP + j] = rate * gradient[i, j] * (1.0 / 12.0)
    at = COMP + COMP * COMP
    for i, j in PAIRS:
        for order in range(3):
            table[at] = interaction[order, i, j]
            at += 1
    copies[0].wait()


def coefficients(table):
    rates = [table[i] for i in range(COMP)]
    mixing = [[table[COMP + i * COMP + j] for j in range(COMP)] for i in range(COMP)]
    at = COMP + COMP * COMP
    pairs = {pair: [table[at + 3 * n + order] for order in range(3)] for n, pair in enumerate(PAIRS)}
    return rates, mixing, pairs


def mixed(start, laps, mixing):
    result = []
    for i in range(COMP):
        total = start[i]
        for j in range(COMP):
            total += mixing[i][j] * laps[j]
        result.append(total)
    return result


def pieces(values):
    rest = jnp.concatenate(values, axis=0)
    result = []
    for n in range(3):
        piece = rest.astype(jnp.bfloat16)
        result.append(piece)
        rest = rest - piece.astype(jnp.float32)
    return result


def steps(chunks, weights, scalars):
    rates, mixing, pairs = scalars
    layer, _, x = lane_parts(chunks[0][0][0].shape)
    slots = chunks[0][0][0].shape[0]
    rows = []
    for v, ahead, behind, above, below, beside in chunks:
        ends = [jnp.where(x < 4, a, b) for a, b in zip(ahead, behind)]
        layers = [jnp.where(layer == 0, a, b) for a, b in zip(above, below)]
        rows += [jnp.concatenate(p, axis=1) for p in zip(*[pieces(part) for part in (v, beside, ends, layers)])]
    sums = jnp.dot(jnp.concatenate(rows, axis=0), weights[...], preferred_element_type=jnp.float32)
    count = COMP * slots
    results = []
    for n, (v, _, _, above, below, _) in enumerate(chunks):
        near = sum(sums[(3 * n + m) * count : (3 * n + m + 1) * count] for m in range(3))
        laps = [near[c * slots : (c + 1) * slots] - (above[c] + below[c]) - 90.0 * v[c] for c in range(COMP)]
        drive = [None] * COMP
        for (i, j), (a, b, c) in pairs.items():
            gap = v[i] - v[j]
            bend = c * gap
            slope = b + bend
            energy = a + slope * gap
            cross = v[i] * v[j] * (slope + bend)
            first = v[j] * energy + cross
            second = v[i] * energy - cross
            drive[i] = first if drive[i] is None else drive[i] + first
            drive[j] = second if drive[j] is None else drive[j] + second
        results.append(mixed([v[i] - rates[i] * drive[i] for i in range(COMP)], laps, mixing))
    return results


def store(slots, ref, at, values):
    for c, value in enumerate(values):
        ref[at, c, TOP : TOP + slots, :] = value
        ref[at, c, TOP - 1 : TOP, :] = value[slots - 1 :]
        ref[at, c, TOP + slots : TOP + slots + 1, :] = value[:1]


def load(slots, ref, at, offset=0):
    return [ref[at, c, TOP + offset : TOP + offset + slots, :] for c in range(COMP)]


def move(slots, work, places, weights, scalars):
    chunks = []
    for at, above, below, beside, _ in places:
        around = [load(slots, work, n) for n in (above, below, beside)]
        chunks.append((load(slots, work, at), load(slots, work, at, 1), load(slots, work, at, -1), *around))
    for place, values in zip(places, steps(chunks, weights, scalars)):
        store(slots, work, place[-1], values)


def column(ref, start, count, stride):
    flat = ref.reshape(ref.shape[0] * ref.shape[1], LANES)
    return flat[pl.ds(start, count, stride=stride), :]


SPAN = CHUNKS + 2
BLOCK, SIDE, BLOCK_NEXT, SIDE_NEXT, FINAL, BEYOND = [n * SPAN for n in range(5)] + [4 * SPAN + 2]
ENTRIES = BEYOND + 2


def inner_kernel(cap, slots, peers, *refs):
    got, (table, weights, work, block, high, low) = refs[: peers // 2], refs[peers // 2 :]
    scalars = coefficients(table)
    _, y, _ = lane_parts((slots, LANES))
    for message, whole, joined, slot, high_slot, low_slot in entries(cap, got):
        block[slot] = message[whole : whole + ROWS, :]
        rows = message[joined : joined + ROWS, :]
        high[high_slot] = rows
        low[low_slot] = rows
    for base in range(0, FINAL, SPAN):
        for at in (base, base + SPAN - 1):
            work[at] = jnp.zeros(work.shape[1:], work.dtype)

    @pl.loop(0, CHUNKS)
    def _(k):
        rows = [k * COMP + c for c in range(COMP)]
        store(slots, work, BLOCK + 1 + k, [column(block, r, slots, ROWS) for r in rows])
        sides = [jnp.where(y < 4, column(high, r, slots, ROWS), column(low, r, slots, ROWS)) for r in rows]
        store(slots, work, SIDE + 1 + k, sides)

    @pl.loop(0, 2)
    def _(side):
        places = []
        for k in range(1, CHUNKS + 1):
            at = side * SPAN + k
            places.append((at, at + 1, at - 1, (1 - side) * SPAN + k, BLOCK_NEXT + at))
        move(slots, work, places, weights, scalars)

    second, third = BLOCK_NEXT + 2, BLOCK_NEXT + 3
    places = [
        (second, third, BLOCK_NEXT, SIDE_NEXT + 2, FINAL),
        (third, BLOCK_NEXT + SPAN - 1, second, SIDE_NEXT + 3, FINAL + 1),
    ]
    move(slots, work, places, weights, scalars)


def outer_kernel(slots, below, above, table, weights, _, out, work, middle, ends, sems):
    scalars = coefficients(table)
    mixing = scalars[1]
    pairs = slots // 2
    last = SPAN - 1
    _, y, _ = lane_parts((pairs, LANES))
    layer, _, _ = lane_parts((slots, LANES))

    def add(start, beyond, end):
        laps = [16.0 * turn(jnp.where(layer == 1 - end, b, 0.0), 64) - b for b in beyond]
        return mixed(start, laps, mixing)

    for end, ref in enumerate((below, above)):
        near, distant, side = [], [], []
        for c in range(COMP):
            near.append(column(ref, (1 - end) * COMP + c, slots, HALF))
            distant.append(column(ref, end * COMP + c, slots, HALF))
            both = column(ref, slots * HALF + c, pairs, COMP)
            side.append(jnp.concatenate([both, second_of(both, y)], axis=0))
        edge = 1 + end * (CHUNKS - 1)
        store(slots, work, BLOCK + end * last, near)
        store(slots, work, BEYOND + end, distant)
        store(slots, work, SIDE + end * last, side)
        first = add(load(slots, work, BLOCK_NEXT + edge), near, end)
        store(slots, work, SIDE_NEXT + edge, add(load(slots, work, SIDE_NEXT + edge), side, end))
        store(slots, work, BLOCK_NEXT + edge, first)
        for c, value in enumerate(add(load(slots, work, FINAL + end), first, end)):
            middle[:, c, end * LANES : (end + 1) * LANES] = value

    copies = [pltpu.make_async_copy(middle, out.at[:, :, LANES : 3 * LANES], sems.at[2])]
    copies[0].start()

    for late in range(2):
        places = []
        for end in range(2):
            outside = end * last
            at = BLOCK_NEXT + 1 + end * (CHUNKS - 1) if late else BLOCK + outside
            beyond = BLOCK_NEXT + outside if late else BEYOND + end
            beside = SIDE_NEXT + 1 + end * (CHUNKS - 1) if late else SIDE + outside
            to = (BLOCK if late else BLOCK_NEXT) + outside
            up, down = (beyond, at - 1) if end else (at + 1, beyond)
            places.append((at, up, down, beside, to))
        move(slots, work, places, weights, scalars)

    for end in range(2):
        for c, value in enumerate(load(slots, work, BLOCK + end * last)):
            ends[end, :, c, :] = value
        at = end * (CHUNKS - 1) * LANES
        copies.append(pltpu.make_async_copy(ends.at[end], out.at[:, :, at : at + LANES], sems.at[end]))
        copies[-1].start()
    for copy in copies:
        copy.wait()


def per_device(fields, target, gradient_matrix, relaxation, interaction):
    slots = fields.shape[0]
    peers = lax.axis_size("loc")
    groups = lax.axis_size("grp")
    cap = (slots + peers - 1) // peers
    chips = peers // 2
    f32 = jnp.float32
    params = pltpu.CompilerParams(vmem_limit_bytes=8 << 20)

    def shape(*dims):
        return pltpu.VMEM(dims, f32)

    def inside(*arrays):
        return [pltpu.with_memory_space_constraint(a, pltpu.VMEM) for a in arrays]

    def cross(array, flip):
        return lax.ppermute(array, "loc", [(i, i ^ flip) for i in range(peers)])

    numbers = pltpu.SMEM((peers * cap,), jnp.int32)
    arguments = fields, target, gradient_matrix, relaxation, interaction
    staged, held, label, table = pl.pallas_call(
        lambda *refs: stage_kernel(peers, cap, slots, *refs),
        out_shape=(shape(*fields.shape), numbers, numbers, pltpu.SMEM((TABLE,), f32)),
        in_specs=[pl.BlockSpec(memory_space=pl.ANY)] * 5,
        out_specs=(VMEM, SMEM, SMEM, SMEM),
        scratch_shapes=[pltpu.SMEM(a.shape, a.dtype) for a in arguments[1:]]
        + [pltpu.SMEM((peers,), jnp.int32), pltpu.SemaphoreType.DMA((5,))],
        name="stage",
    )(*arguments)
    table = pltpu.with_memory_space_constraint(table, pltpu.SMEM)
    other_fields, other_target = cross(fields, 1), cross(target.reshape(1, slots), 1)
    other = pl.pallas_call(
        lambda *refs: other_route_kernel(peers, cap, slots, *refs),
        out_shape=(numbers, numbers),
        in_specs=[VMEM],
        out_specs=(SMEM,) * 2,
        scratch_shapes=[pltpu.SMEM((peers,), jnp.int32)],
        name="route",
        compiler_params=params,
    )(*inside(other_target))
    routes = [pltpu.with_memory_space_constraint(a, pltpu.SMEM) for a in (held, label, *other)]

    def pack(flip):
        message = shape(4 * cap * ROWS + 8, LANES)
        extra = () if flip else (pltpu.VMEM((4 * LANES, LANES), jnp.bfloat16),)
        return pl.pallas_call(
            lambda *refs: pack_kernel(peers, cap, flip, *refs),
            out_shape=(message, *extra),
            in_specs=[SMEM] * 4 + [VMEM] * 2,
            out_specs=(VMEM,) * (1 + len(extra)),
            name="pack",
            compiler_params=params,
        )(*routes, *inside(staged, other_fields))

    flips = [2 * j + 1 for j in reversed(range(1, chips))] + [0]
    *sent, (own, weights) = [pack(flip) for flip in flips]
    weights = inside(weights)[0]
    got = inside(*[cross(message, flip) for (message,), flip in zip(sent, flips)], own)
    early, late = got[: chips // 2 - 1] + got[-1:], got[chips // 2 - 1 : -1]
    counts = len(early), len(late)
    face, corner = (slots + slots // 4, HALF, LANES), ((slots + 2) * COMP, LANES)
    corners = shape(*face), shape(*corner), shape(*corner)
    up_early, *down = pl.pallas_call(
        lambda *refs: early_kernel(cap, counts[0], *refs),
        out_shape=(shape(bundle_rows(cap, counts[0])[-1], LANES), *corners),
        in_specs=[VMEM] * counts[0],
        out_specs=(VMEM,) * 4,
        name="early",
        compiler_params=params,
    )(*early)
    up_late = shape(bundle_rows(cap, counts[1])[-1], LANES)
    going = pl.pallas_call(
        lambda *refs: next_kernel(cap, *refs),
        out_shape=(up_late, *corners),
        in_specs=[VMEM] * (counts[1] + 2),
        out_specs=(VMEM,) * 4,
        input_output_aliases={counts[1] - 1 + n: 1 + n for n in range(3)},
        name="next",
        compiler_params=params,
    )(*late[:-1], *inside(*down))
    up_late, down, *_ = pl.pallas_call(
        lambda *refs: last_kernel(cap, slots, counts[1], *refs),
        out_shape=(up_late, *corners),
        in_specs=[VMEM] * 5,
        out_specs=(VMEM,) * 4,
        input_output_aliases={1 + n: n for n in range(4)},
        name="last",
        compiler_params=params,
    )(late[-1], *inside(*going))
    forward = [(i, (i + 1) % groups) for i in range(groups)]
    backward = [(j, i) for i, j in forward]
    from_below = [lax.ppermute(up, "grp", forward) for up in (up_early, up_late)]
    above = lax.ppermute(down, "grp", backward)
    below = pl.pallas_call(
        lambda *refs: catch_kernel(cap, slots, counts, *refs),
        out_shape=shape(*face),
        in_specs=[VMEM],
        out_specs=VMEM,
        scratch_shapes=[pltpu.VMEM(corner, f32)] * 2,
        name="catch",
        compiler_params=params,
    )(*inside(jnp.concatenate(from_below)))
    work = pl.pallas_call(
        lambda *refs: inner_kernel(cap, slots, peers, *refs),
        out_shape=shape(ENTRIES, COMP, DEPTH, LANES),
        in_specs=[VMEM] * chips + [SMEM, VMEM],
        out_specs=VMEM,
        scratch_shapes=[pltpu.VMEM((slots + 1, ROWS, LANES), f32)] * 3,
        name="inner",
        compiler_params=params,
    )(*got, table, weights)
    return pl.pallas_call(
        lambda *refs: outer_kernel(slots, *refs),
        out_shape=(jax.ShapeDtypeStruct(fields.shape, f32), shape(*work.shape)),
        in_specs=[VMEM] * 2 + [SMEM] + [VMEM] * 2,
        out_specs=(pl.BlockSpec(memory_space=pl.ANY), VMEM),
        input_output_aliases={4: 1},
        scratch_shapes=[
            pltpu.VMEM((slots, COMP, 2 * LANES), f32),
            pltpu.VMEM((2, slots, COMP, LANES), f32),
            pltpu.SemaphoreType.DMA((3,)),
        ],
        name="outer",
        compiler_params=params,
    )(*inside(below, above), table, weights, *inside(work))[0]


def solution(mesh):
    placed = (P(("grp", "loc"), None, None), P(("grp", "loc")), P(), P(), P())
    return jax.shard_map(
        per_device,
        mesh=mesh,
        in_specs=placed,
        out_specs=P(("grp", "loc"), None, None),
        check_vma=False,
    )
```
